128 devices in a mesh: tok: 16 (over y, x), exp: 8 (over z, core).
Axes of the slice: x: 4, y: 4, z: 4, core: 2. Of those that a mesh axis runs over, the one named last changes fastest.
Arguments:
- x_var: bfloat16 [48, 16, 1024, 1024], P('tok', None, 'exp'), may hold values from -40 to 40
- var_ids: int32 [48], P('tok'), may hold values from 0 to 47, each once
- var_embed: bfloat16 [48, 1024], replicated, may hold values from -3 to 3
- score_vecs: bfloat16 [1024, 16], replicated, may hold values from -0.1875 to 0.1875
- v_weight: bfloat16 [1024, 1024], replicated, may hold values from -0.1875 to 0.1875
- out_weight: bfloat16 [1024, 1024], replicated, may hold values from -0.1875 to 0.1875
- second_half: bfloat16 [16384, 1024], P(('tok', 'exp')), may hold values from -6 to 6
- norm_gain: bfloat16 [1024], replicated, may hold values from 0.099609375 to 1.8984375
- routes: int32 [16384, 2], P(('tok', 'exp')), may hold values from 0 to 63, all different within a row; in each aligned block of 128 rows (0 to 127, 128 to 255, ...) at most 7 rows name the same one
- route_weights: float32 [16384, 2], P(('tok', 'exp')), may hold values from 0.2 to 1
- w_gate: bfloat16 [64, 1024, 2048], P('tok', None, 'exp'), may hold values from -0.1875 to 0.1875
- w_up: bfloat16 [64, 1024, 2048], P('tok', None, 'exp'), may hold values from -0.1875 to 0.1875
- w_down: bfloat16 [64, 2048, 1024], P('tok', 'exp'), may hold values from -0.125 to 0.125
Outputs:
- blended: bfloat16 [16384, 1024], P(('tok', 'exp'))
The draws below stay inside these ranges and needn't reach their ends.
Inputs may be any that keep to these rules, and one draw needn't show every extreme that they name: `routes`: in the rows of one device no expert is named more than 7 times, and in some device some expert is named exactly 7 times; every token names two different experts.
All inputs are finite; a program needn't handle non-finite values.
Results may differ from the reference program's by a relative error of at most 0.018.
Values may be sent and summed in bfloat16 or wider, within the bound.
A program may use at most 192 MiB of HBM per device.

```python
import math
import jax
import jax.numpy as jnp
import numpy as np
from jax import lax

D = 1024
V = 48
H = 16
HD = 64
EXPERTS = 64
FF = 2048
TOK_DEV = 128
CAP = 7
TOKENS = 16384
N_TOK = 16
N_EXP = 8
DEVICES = 128


def shared_columns(key):
    return jnp.clip(jax.random.normal(key, (D, H), jnp.float32), -4.0, 4.0)


def draw_score_vecs(key, part):
    columns = shared_columns(key)
    return (1.5 * columns / math.sqrt(D)).astype(jnp.bfloat16)


def draw_x_var(key, part):
    key = jax.random.fold_in(key, 23)
    base_key = jax.random.fold_in(key, 0)
    shape = (V, N_TOK, TOK_DEV * N_EXP, D)
    base = jax.random.normal(base_key, shape, jnp.float32)
    return jnp.clip(base, -40.0, 40.0).astype(jnp.bfloat16)


def block_levels(rng, shape, cuts, least, top_value):
    def one(axis_at, shards_of):
        steps = jax.random.uniform(jax.random.fold_in(jax.random.fold_in(rng, 6), axis_at), (shards_of,), jnp.float32, least / len(cuts), top_value / len(cuts))
        return jnp.repeat(jnp.exp(steps), shape[axis_at] // shards_of).reshape((-1,) + (1,) * (len(shape) - axis_at - 1))

    level = one(*cuts[0])
    for cut in cuts[1:]:
        level = level * one(*cut)
    return level


def shared_out(key, own, number, rows, number_of, top, bound, lean):
    sequence = jax.random.permutation(key, number_of)
    crowded, usual = portions_of(number_of, rows * top, bound, lean, True), portions_of(number_of, rows * top, bound, lean, False)
    places = jnp.arange(number_of)

    def named(tallies, offset_by):
        used = int((tallies > 0).sum())
        fixed = max(1, used // 4)
        shifted = fixed + (places - fixed + offset_by * (used - fixed)) % max(1, number_of - fixed)
        return jnp.zeros((number_of,), jnp.int32).at[sequence[jnp.where(places < fixed, places, shifted)]].set(jnp.asarray(tallies, jnp.int32))

    tallies = jnp.where(number % 4 == 0, named(crowded, number // 4), named(usual, number - number // 4 - 1))
    mixed = jax.random.permutation(jax.random.fold_in(own, 3), number_of)
    donor, taker = mixed[0:number_of // 2 * 2:2], mixed[1:number_of // 2 * 2:2]
    margin = jnp.minimum(tallies[donor] - 1, bound - tallies[taker]) // 2
    margin = jnp.where((donor == sequence[0]) | (taker == sequence[0]) | (tallies[taker] == 0), 0, jnp.maximum(margin, 0))
    shifted = jax.random.randint(jax.random.fold_in(own, 4), (number_of // 2,), 0, 1 << 20) % (margin + 1)
    tallies = tallies.at[donor].add(-shifted).at[taker].add(shifted)
    members = jnp.searchsorted(jnp.cumsum(tallies), jnp.arange(rows * top), side="right").astype(jnp.int32)
    table = members.reshape(top, rows).T
    table = table[jax.random.permutation(jax.random.fold_in(own, 1), rows)]
    offset_by = jax.random.randint(jax.random.fold_in(own, 2), (rows, 1), 0, top)
    return jnp.take_along_axis(table, (jnp.arange(top)[None, :] + offset_by) % top, axis=1)


def portions_of(number_of, total, most, lean, full):
    loads = [(1 << 20) // math.isqrt(rank ** lean) + 1 for rank in range(1, number_of + 1)]
    largest = most if full else min(most, max(-(-total // number_of), total * loads[0] // sum(loads)))
    least = 1 if total - largest >= number_of - 1 else 0
    counts, surplus = [largest] + [least] * (number_of - 1), total - largest - least * (number_of - 1)
    while surplus > 0:
        free = [i for i in range(1, number_of) if counts[i] < largest] or [i for i in range(1, number_of) if counts[i] < most]
        whole, budget = sum([loads[i] for i in free]), surplus
        for i in free:
            addition = min(most - counts[i], max(1, budget * loads[i] // whole), surplus)
            counts[i] = counts[i] + addition
            surplus = surplus - addition
    return np.array(counts)


def gaussian(key, extent, scale, limit, cuts=(), held_as=jnp.bfloat16):
    drawn = jax.random.normal(key, extent, jnp.float32) * scale
    if len(cuts) > 0:
        drawn = block_levels(key, extent, cuts, -0.22, 0.18) * drawn
    return jnp.clip(drawn, min=-limit, max=limit).astype(held_as)


def setup_inputs(seed: int = 0) -> dict:
    arg_keys = jax.random.split(jax.random.key(seed), 14)
    x_var = draw_x_var(jax.random.fold_in(arg_keys[13], 71), 0)
    var_ids = jax.random.permutation(arg_keys[1], V).astype(jnp.int32)
    var_embed = gaussian(arg_keys[2], (V, D), 0.5, 3.0)
    score_vecs = draw_score_vecs(jax.random.fold_in(arg_keys[13], 71), 0)
    v_weight = gaussian(arg_keys[4], (D, D), D ** -0.5, 0.1875)
    out_weight = gaussian(arg_keys[5], (D, D), D ** -0.5, 0.1875)
    second_half = gaussian(arg_keys[6], (TOKENS, D), 1.0, 6.0, ((0, 128),))
    norm_gain = jnp.clip(1.0 + 0.18 * jax.random.normal(arg_keys[7], (D,), jnp.float32), 0.099609375, 1.8984375).astype(jnp.bfloat16)
    routes_keys = jax.random.split(jax.random.fold_in(arg_keys[8], 1), TOKENS // TOK_DEV)
    routes_turns = jax.random.permutation(jax.random.fold_in(arg_keys[8], 3), TOKENS // TOK_DEV)
    routes = jax.vmap(lambda own, number: shared_out(jax.random.fold_in(arg_keys[8], 2), own, number, TOK_DEV, EXPERTS, 2, CAP, 2))(routes_keys, routes_turns).reshape((TOKENS, 2))
    route_weights = jnp.clip(0.2 + 0.8 * jax.random.uniform(arg_keys[9], (TOKENS, 2), jnp.float32) ** block_levels(arg_keys[9], (TOKENS, 2), ((0, 128),), -0.2, 0.2), 0.2, 1.0)
    w_gate = gaussian(arg_keys[10], (EXPERTS, D, FF), D ** -0.5, 0.1875, ((0, 16), (2, 8)))
    w_up = gaussian(arg_keys[11], (EXPERTS, D, FF), D ** -0.5, 0.1875, ((0, 16), (2, 8)))
    w_down = gaussian(arg_keys[12], (EXPERTS, FF, D), FF ** -0.5, 0.125, ((0, 16), (1, 8)))
    return dict(x_var=x_var, var_ids=var_ids, var_embed=var_embed, score_vecs=score_vecs, v_weight=v_weight, out_weight=out_weight, second_half=second_half, norm_gain=norm_gain, routes=routes, route_weights=route_weights, w_gate=w_gate, w_up=w_up, w_down=w_down)


def aggregate_block(block, score_vecs, value_heads):
    embedded = block.astype(jnp.float32)
    scores = jnp.einsum('vtd,dh->vth', embedded, score_vecs.astype(jnp.float32))
    peak = lax.optimization_barrier(jnp.max(scores, axis=0))
    expo = jnp.exp(scores - peak[None])
    denom = lax.optimization_barrier(jnp.sum(expo, axis=0))
    attn_weights = expo.astype(jnp.bfloat16).astype(jnp.float32)
    mixture = jnp.einsum('vth,vtd->thd', attn_weights, embedded)
    heads = jnp.einsum('thd,dhj->thj', mixture, value_heads, precision=lax.Precision.HIGHEST)
    heads = heads / denom[..., None]
    return heads.reshape(heads.shape[0], -1).astype(jnp.bfloat16)

def expert_apply(packed):
    rows, gate_w, up_w, down_w = packed
    gate = jnp.dot(rows, gate_w, preferred_element_type=jnp.float32)
    up = jnp.dot(rows, up_w, preferred_element_type=jnp.float32)
    hidden = (jax.nn.silu(gate) * up).astype(jnp.bfloat16)
    width = hidden.shape[1] // N_EXP
    split_hidden = hidden.reshape(hidden.shape[0], N_EXP, width).astype(jnp.float32)
    split_down = down_w.reshape(N_EXP, width, down_w.shape[1]).astype(jnp.float32)
    partial_out = jnp.einsum('rsf,sfd->srd', split_hidden, split_down)
    partial_out = partial_out.astype(jnp.bfloat16).astype(jnp.float32)
    return lax.optimization_barrier(jnp.sum(partial_out, axis=0)).astype(jnp.bfloat16)

def reference(x_var, var_ids, var_embed, score_vecs, v_weight, out_weight, second_half, norm_gain, routes, route_weights, w_gate, w_up, w_down):
    flat_x = x_var.reshape(V, TOKENS, D)
    labels = var_embed[var_ids].astype(jnp.float32)
    embedded = (flat_x.astype(jnp.float32) + labels[:, None, :]).astype(jnp.bfloat16)
    block_rows = min(512, TOKENS)
    blocks = TOKENS // block_rows
    blocked = jnp.moveaxis(embedded.reshape(V, blocks, block_rows, D), 1, 0)
    value_heads = v_weight.astype(jnp.float32).reshape(D, H, HD)
    heads = lax.map(lambda block: aggregate_block(block, score_vecs, value_heads), blocked)
    heads = heads.reshape(TOKENS, D)
    cross = jnp.dot(heads, out_weight, preferred_element_type=jnp.float32)
    level = second_half.astype(jnp.float32)
    scale = lax.rsqrt(lax.optimization_barrier(jnp.mean(level * level, axis=-1, keepdims=True)) + 1e-06)
    normed = (level * scale * norm_gain.astype(jnp.float32)).astype(jnp.bfloat16)
    device_routes = routes.reshape(DEVICES, TOK_DEV * 2)
    picks = (device_routes[:, :, None] == jnp.arange(EXPERTS, dtype=jnp.int32)[None, None, :]).astype(jnp.int32)
    earlier = jnp.cumsum(picks, axis=1) - picks
    slots = lax.optimization_barrier(jnp.sum(earlier * picks, axis=2)).reshape(-1).astype(jnp.int32)
    flat_ids = device_routes.reshape(-1).astype(jnp.int32)
    devices_of = (jnp.arange(TOKENS * 2, dtype=jnp.int32) // (TOK_DEV * 2)).astype(jnp.int32)
    repeated = jnp.repeat(normed, 2, axis=0)
    buffer = jnp.zeros((EXPERTS, DEVICES, CAP, D), jnp.bfloat16)
    buffer = buffer.at[flat_ids, devices_of, slots].set(repeated)
    buffer = buffer.reshape(EXPERTS, DEVICES * CAP, D)
    expert_out = lax.map(expert_apply, (buffer, w_gate, w_up, w_down))
    picked = expert_out[flat_ids, devices_of * CAP + slots].astype(jnp.float32)
    picked = picked.reshape(TOKENS, 2, D)
    moe = lax.optimization_barrier(jnp.sum(picked * route_weights[..., None], axis=1))
    return (cross + moe).astype(jnp.bfloat16)
```

```python
import jax
import jax.numpy as jnp
from jax import lax
from jax.sharding import PartitionSpec as P

EXPERTS = 64
CAP = 7


def add_labels(x_var, var_ids, var_embed):
    count = var_embed.shape[0]
    picks = (var_ids[:, None] == jnp.arange(count, dtype=jnp.int32)[None, :]).astype(jnp.bfloat16)
    labels = jnp.dot(picks, var_embed, preferred_element_type=jnp.float32)
    shaped = labels.reshape((labels.shape[0], 1, 1, labels.shape[1]))
    return (x_var.astype(jnp.float32) + shaped).astype(jnp.bfloat16)


def aggregate(x_var, var_ids, var_embed, score_vecs, v_weight, out_weight):
    width = x_var.shape[3]
    heads_count = score_vecs.shape[1]
    embedded = add_labels(x_var, var_ids, var_embed)
    scores = jnp.einsum("vntd,dh->vnth", embedded, score_vecs, preferred_element_type=jnp.float32)
    peak = lax.pmax(jnp.max(scores, axis=0), "tok")
    values = jnp.einsum(
        "vntd,dk->vntk", embedded, v_weight, preferred_element_type=jnp.float32
    ).astype(jnp.bfloat16)
    expo = jnp.exp(scores - peak[None])
    denom = lax.psum_scatter(jnp.sum(expo, axis=0), "tok", scatter_dimension=0, tiled=True)
    spread = (
        jnp.arange(heads_count)[:, None] == jnp.arange(width)[None, :] // (width // heads_count)
    ).astype(jnp.bfloat16)
    weights = jnp.einsum(
        "vnth,hk->vntk", expo.astype(jnp.bfloat16), spread, preferred_element_type=jnp.float32
    ).astype(jnp.bfloat16)
    mixed = jnp.sum(weights.astype(jnp.float32) * values.astype(jnp.float32), axis=0)
    mixed = lax.psum_scatter(
        mixed.astype(jnp.bfloat16), "tok", scatter_dimension=0, tiled=True
    )[0].astype(jnp.float32)
    inverse = jnp.repeat(1.0 / denom[0], width // heads_count, axis=1)
    heads = (mixed * inverse).astype(jnp.bfloat16)
    return jnp.dot(heads, out_weight, preferred_element_type=jnp.float32)


def experts_path(second_half, norm_gain, routes, route_weights, w_gate, w_up, w_down):
    tok_rows, width = second_half.shape
    level = second_half.astype(jnp.float32)
    scale = lax.rsqrt(jnp.mean(level * level, axis=-1, keepdims=True) + 1e-06)
    normed = (level * scale * norm_gain.astype(jnp.float32)).astype(jnp.bfloat16)
    flat_ids = routes.reshape(-1)
    picks = (flat_ids[:, None] == jnp.arange(EXPERTS, dtype=jnp.int32)[None, :]).astype(jnp.int32)
    earlier = jnp.cumsum(picks, axis=0) - picks
    slots = jnp.sum(earlier * picks, axis=1)
    target = flat_ids * CAP + slots
    repeated = jnp.repeat(normed, 2, axis=0)
    placing = (target[None, :] == jnp.arange(EXPERTS * CAP, dtype=jnp.int32)[:, None]).astype(
        jnp.bfloat16
    )
    packed = jnp.dot(placing, repeated, preferred_element_type=jnp.float32).astype(jnp.bfloat16)
    groups = lax.axis_size("tok")
    packed = packed.reshape(groups, EXPERTS // groups, CAP, width)
    arrived = lax.all_to_all(packed, "tok", split_axis=0, concat_axis=0, tiled=True)
    piece = lax.all_gather(arrived, "exp", axis=0, tiled=True)
    gate = jnp.einsum("secd,edf->secf", piece, w_gate, preferred_element_type=jnp.float32)
    up = jnp.einsum("secd,edf->secf", piece, w_up, preferred_element_type=jnp.float32)
    hidden = (jax.nn.silu(gate) * up).astype(jnp.bfloat16)
    partial_out = jnp.einsum("secf,efd->secd", hidden, w_down, preferred_element_type=jnp.float32)
    summed = lax.psum_scatter(
        partial_out.astype(jnp.bfloat16), "exp", scatter_dimension=0, tiled=True
    )
    returned = lax.all_to_all(summed, "tok", split_axis=0, concat_axis=0, tiled=True)
    results = returned.reshape(EXPERTS * CAP, width)
    picked = jnp.take(results, target, axis=0).reshape(tok_rows, 2, width).astype(jnp.float32)
    return jnp.sum(picked * route_weights[..., None], axis=1)


def shards(
    x_var,
    var_ids,
    var_embed,
    score_vecs,
    v_weight,
    out_weight,
    second_half,
    norm_gain,
    routes,
    route_weights,
    w_gate,
    w_up,
    w_down,
):
    cross = aggregate(x_var, var_ids, var_embed, score_vecs, v_weight, out_weight)
    moe = experts_path(second_half, norm_gain, routes, route_weights, w_gate, w_up, w_down)
    return (cross + moe).astype(jnp.bfloat16)


def solution(mesh):
    in_specs = (
        P("tok", None, "exp", None),
        P("tok"),
        P(),
        P(),
        P(),
        P(),
        P(("tok", "exp"), None),
        P(),
        P(("tok", "exp"), None),
        P(("tok", "exp"), None),
        P("tok", None, "exp"),
        P("tok", None, "exp"),
        P("tok", "exp", None),
    )
    out_specs = P(("tok", "exp"), None)
    return jax.shard_map(shards, mesh=mesh, in_specs=in_specs, out_specs=out_specs, check_vma=False)
```

```python
import jax
import jax.numpy as jnp
from jax import lax
from jax.experimental import pallas as pl
from jax.experimental.pallas import tpu as pltpu
from jax.sharding import PartitionSpec as P

MESH = pl.DeviceIdType.MESH
BF16 = jnp.bfloat16
F32 = jnp.float32
D = 1024
H = 16
VARS = 3
ROWS = 128
EXPERTS = 64
GROUP = 4
FF = 256
CAP = 7
NT = 16
NZ = 4
BLK = NT * CAP
HALF = NZ * BLK
PAIR = NT * 16
XSLOTS = 3


def dot(a, b):
    return jnp.dot(a, b, preferred_element_type=F32)


def dot_t(a, b):
    return lax.dot_general(a, b, (((0,), (0,)), ((), ())), preferred_element_type=F32)


def iota(shape, dim):
    return lax.broadcasted_iota(jnp.int32, shape, dim)


def kernel(
    x,
    ids,
    embed,
    svec,
    vw,
    ow,
    half,
    gain,
    routes,
    rweights,
    wg,
    wu,
    wd,
    out,
    wgu,
    wdn,
    vwb,
    owb,
    xbuf,
    lab,
    svt,
    spread,
    chi,
    clo,
    pk,
    rb,
    ag,
    pt,
    sb,
    zr1,
    zr2,
    so,
    rs,
    rr,
    ns,
    nr,
    st_s,
    st_r,
    acc,
    xsem,
    wsem,
    a_s,
    a_r,
    g_s,
    g_r,
    p_s,
    p_r,
    r_s,
    r_r,
    n_s,
    n_r,
    t_s,
    t_r,
    own_sem,
):
    me = lax.axis_index("tok")
    ex = lax.axis_index("exp")
    z = ex // 2
    core = ex % 2
    up = (me, ((z + 1) % NZ) * 2 + core)
    down = (me, ((z + NZ - 1) % NZ) * 2 + core)
    sib = (me, z * 2 + (1 - core))

    def tok_dev(o):
        return ((me + o) % NT, ex)

    def remote(src, dst, send, recv, dev):
        return pltpu.make_async_remote_copy(
            src_ref=src, dst_ref=dst, send_sem=send, recv_sem=recv, device_id=dev, device_id_type=MESH
        )

    def rows_at(start, size):
        return pl.ds(pl.multiple_of(start, 16), size)

    def x_copy(o):
        slot = o % XSLOTS
        return pltpu.make_async_copy(x.at[:, (me + o) % NT], xbuf.at[slot], xsem.at[slot])

    vw_copy = pltpu.make_async_copy(vw, vwb, wsem.at[0])
    ow_copy = pltpu.make_async_copy(ow, owb, wsem.at[1])
    w_copies = []
    for e in range(GROUP):
        w_copies.append(
            (
                pltpu.make_async_copy(wg.at[e], wgu.at[e, :, 0:FF], wsem.at[2 + 3 * e]),
                pltpu.make_async_copy(wu.at[e], wgu.at[e, :, FF : 2 * FF], wsem.at[3 + 3 * e]),
                pltpu.make_async_copy(wd.at[e], wdn.at[e], wsem.at[4 + 3 * e]),
            )
        )

    barrier = pltpu.get_barrier_semaphore()
    greeted = [tok_dev(o) for o in range(1, NT)] + [up, down, sib]
    for dev in greeted:
        pl.semaphore_signal(barrier, inc=1, device_id=dev, device_id_type=MESH)

    vw_copy.start()
    for o in range(1, 1 + XSLOTS):
        x_copy(o).start()
    for group in w_copies:
        for copy in group:
            copy.start()
    ow_copy.start()

    level = half[...].astype(F32)
    scale = lax.rsqrt(jnp.mean(level * level, axis=-1, keepdims=True) + 1e-06)
    normed = (level * scale * gain[...].astype(F32)).astype(BF16)
    route0 = routes[:, 0:1]
    route1 = routes[:, 1:2]
    experts = iota((ROWS, EXPERTS), 1)
    named0 = route0 == experts
    named1 = route1 == experts
    either = jnp.where(named0 | named1, 1.0, 0.0).astype(BF16)
    before = jnp.where(iota((ROWS, ROWS), 0) > iota((ROWS, ROWS), 1), 1.0, 0.0).astype(BF16)
    count = dot(before, either)

    def target(route, named):
        slot = jnp.sum(jnp.where(named, count, 0.0), axis=1, keepdims=True).astype(jnp.int32)
        pair = jnp.right_shift(route, 1) & 1
        return pair * PAIR + jnp.right_shift(route, 2) * 16 + (route & 1) * 8 + slot

    places = iota((ROWS, 2 * PAIR), 1)
    here0 = places == target(route0, named0)
    here1 = places == target(route1, named1)
    placing = jnp.where(here0 | here1, 1.0, 0.0).astype(BF16)
    pk[...] = dot_t(placing, normed).astype(BF16)
    weights = jnp.where(here0, rweights[:, 0:1], 0.0) + jnp.where(here1, rweights[:, 1:2], 0.0)
    high = weights.astype(BF16)
    chi[...] = high
    clo[...] = (weights - high.astype(F32)).astype(BF16)

    pl.semaphore_wait(barrier, len(greeted))

    def dispatch(p, o):
        mine = rows_at(p * PAIR + me * 16, 16)
        theirs = rows_at(p * PAIR + ((me + o) % NT) * 16, 16)
        return remote(pk.at[theirs], rb.at[mine], a_s.at[p, o], a_r.at[p, o], tok_dev(o))

    for p in range(2):
        for o in range(1, NT):
            dispatch(p, o).start()

    def dispatch_arrived(p):
        mine = rows_at(p * PAIR + me * 16, 16)
        rb[mine] = pk[mine]
        for o in range(1, NT):
            dispatch(p, o).wait_recv()

    picks = jnp.where(ids[...] == iota((VARS, embed.shape[0]), 1), 1.0, 0.0).astype(BF16)
    lab[0:VARS] = dot(picks, embed[...])
    svt[...] = jnp.transpose(svec[...].astype(F32)).astype(BF16)
    spread[...] = jnp.where(jnp.right_shift(iota((H, D), 1), 6) == iota((H, D), 0), 1.0, 0.0).astype(BF16)
    vw_copy.wait()

    def sum_copy(o):
        dest = (me + o) % NT
        return remote(ns.at[dest], nr.at[me], n_s.at[o], n_r.at[o], tok_dev(o))

    def stat_copy(o):
        dest = (me + o) % NT
        return remote(st_s.at[dest], st_r.at[me], t_s.at[o], t_r.at[o], tok_dev(o))

    def aggregate(o, _):
        dest = (me + o) % NT
        slot = o % XSLOTS
        x_copy(o).wait()
        embedded = jnp.concatenate(
            [(xbuf[slot, v].astype(F32) + lab[v : v + 1]).astype(BF16) for v in range(VARS)], axis=0
        )
        scores = lax.dot_general(
            svt[...], embedded, (((1,), (1,)), ((), ())), preferred_element_type=F32
        )
        parts = [scores[:, v * ROWS : (v + 1) * ROWS] for v in range(VARS)]
        peak = jnp.maximum(jnp.maximum(parts[0], parts[1]), parts[2])
        expo = [jnp.exp(part - peak) for part in parts]
        denom = expo[0] + expo[1] + expo[2]
        inverse = 1.0 / denom
        st_s[dest, 0:H] = peak
        st_s[dest, H : 2 * H] = denom
        values = dot(embedded, vwb[...])
        mixed = None
        for v in range(VARS):
            share = dot_t((expo[v] * inverse).astype(BF16), spread[...])
            term = share * values[v * ROWS : (v + 1) * ROWS]
            mixed = term if mixed is None else mixed + term
        ns[dest] = mixed.astype(BF16)

        @pl.when(o < NT)
        def _():
            sum_copy(o).start()
            stat_copy(o).start()

        @pl.when(o + XSLOTS <= NT)
        def _():
            x_copy(o + XSLOTS).start()

        return 0

    def aggregate_range(low, high_):
        lax.fori_loop(low, high_, aggregate, 0)

    def packed_row(col):
        return (jnp.right_shift(col, 3) & 1) * BLK + jnp.right_shift(col, 4) * CAP + (col & 7)

    mine_ag = (core * NZ + z) * BLK

    def compact(p):
        col = iota((2 * BLK, PAIR), 1)
        pick = jnp.where(
            (iota((2 * BLK, PAIR), 0) == packed_row(col)) & ((col & 7) < CAP), 1.0, 0.0
        ).astype(BF16)
        dense = dot(pick, rb[p * PAIR : (p + 1) * PAIR]).astype(BF16)
        ag[2 * p, rows_at(mine_ag, BLK)] = dense[0:BLK]
        ag[2 * p + 1, rows_at(mine_ag, BLK)] = dense[BLK : 2 * BLK]

    def low_rows(e):
        return 64 if e % 2 == 0 else 48

    def block_row(c, dz):
        return (c * NZ + (z + dz) % NZ) * BLK

    def gather_copy(e, kind):
        low = low_rows(e)
        start, size, dev = {
            0: (block_row(core, 0), BLK, up),
            1: (block_row(core, 0), BLK, down),
            2: (block_row(core, NZ - 1), low, up),
            3: (block_row(core, 1) + low, BLK - low, down),
            4: (block_row(core, 0), BLK, sib),
            5: (block_row(core, NZ - 1), BLK, sib),
            6: (block_row(core, 1), BLK, sib),
            7: (block_row(core, 2), low, sib),
            8: (block_row(core, 2) + low, BLK - low, sib),
        }[kind]
        place = ag.at[e, rows_at(start, size)]
        return remote(place, place, g_s.at[e, kind], g_r.at[e, kind], dev)

    def gather_recv(e, kind):
        low = low_rows(e)
        start, size, dev = {
            0: (block_row(core, NZ - 1), BLK, down),
            1: (block_row(core, 1), BLK, up),
            2: (block_row(core, 2), low, down),
            3: (block_row(core, 2) + low, BLK - low, up),
            4: (block_row(1 - core, 0), BLK, sib),
            5: (block_row(1 - core, NZ - 1), BLK, sib),
            6: (block_row(1 - core, 1), BLK, sib),
            7: (block_row(1 - core, 2), low, sib),
            8: (block_row(1 - core, 2) + low, BLK - low, sib),
        }[kind]
        place = ag.at[e, rows_at(start, size)]
        remote(place, place, g_s.at[e, kind], g_r.at[e, kind], dev).wait_recv()

    def gather_first(e):
        gather_copy(e, 0).start()
        gather_copy(e, 1).start()
        gather_copy(e, 4).start()

    def gather_second(e):
        gather_recv(e, 0)
        gather_copy(e, 2).start()
        gather_copy(e, 5).start()
        gather_recv(e, 1)
        gather_copy(e, 3).start()
        gather_copy(e, 6).start()

    def gather_third(e):
        gather_recv(e, 2)
        gather_copy(e, 7).start()
        gather_recv(e, 3)
        gather_copy(e, 8).start()

    def ffn(e, start):
        rows = rows_at(start, HALF)
        both = dot(ag[e, rows], wgu[e])
        gate = both[:, 0:FF]
        hidden = (gate / (1.0 + jnp.exp(-gate)) * both[:, FF : 2 * FF]).astype(BF16)
        pt[e, rows] = dot(hidden, wdn[e]).astype(BF16)

    def sibling_copy(e):
        return remote(
            pt.at[e, rows_at((1 - core) * HALF, HALF)], sb.at[e], p_s.at[e, 0], p_r.at[e, 0], sib
        )

    def experts_of(e):
        for copy in w_copies[e]:
            copy.wait()
        ffn(e, core * HALF)
        for kind in range(4, 9):
            gather_recv(e, kind)
        ffn(e, (1 - core) * HALF)
        sibling_copy(e).start()

    def part(e, dz, start, size):
        return pt.at[e, rows_at(block_row(core, dz) + start, size)]

    def sum_step(e, kind):
        low = low_rows(e)
        src, dst, dev = {
            1: (part(e, 2, 0, low), zr1.at[e, 0, 0:low], up),
            2: (part(e, 2, low, BLK - low), zr1.at[e, 1, 0 : BLK - low], down),
            3: (part(e, 1, low, BLK - low), zr2.at[e, 0, low:BLK], up),
            4: (part(e, 1, 0, low), zr2.at[e, 0, 0:low], up),
            5: (part(e, NZ - 1, 0, low), zr2.at[e, 1, 0:low], down),
            6: (part(e, NZ - 1, low, BLK - low), zr2.at[e, 1, low:BLK], down),
        }[kind]
        return remote(src, dst, p_s.at[e, kind], p_r.at[e, kind], dev)

    def add_sibling(e, dz):
        here = rows_at(block_row(core, dz), BLK)
        there = rows_at(((z + dz) % NZ) * BLK, BLK)
        pt[e, here] = (pt[e, here].astype(F32) + sb[e, there].astype(F32)).astype(BF16)

    def sum_first(e):
        sibling_copy(e).wait_recv()
        add_sibling(e, 2)
        sum_step(e, 1).start()
        sum_step(e, 2).start()
        add_sibling(e, 1)
        sum_step(e, 3).start()
        add_sibling(e, NZ - 1)
        sum_step(e, 5).start()
        add_sibling(e, 0)

    def sum_second(e):
        low = low_rows(e)
        sum_step(e, 1).wait_recv()
        here = rows_at(block_row(core, 1), low)
        pt[e, here] = (pt[e, here].astype(F32) + zr1[e, 0, 0:low].astype(F32)).astype(BF16)
        sum_step(e, 4).start()
        sum_step(e, 2).wait_recv()
        here = rows_at(block_row(core, NZ - 1) + low, BLK - low)
        pt[e, here] = (pt[e, here].astype(F32) + zr1[e, 1, 0 : BLK - low].astype(F32)).astype(BF16)
        sum_step(e, 6).start()

    def sum_third(e):
        for kind in range(3, 7):
            sum_step(e, kind).wait_recv()
        here = rows_at(block_row(core, 0), BLK)
        total = pt[e, here].astype(F32) + zr2[e, 0].astype(F32) + zr2[e, 1].astype(F32)
        start = (e % 2) * BLK
        so[e // 2, start : start + BLK] = total.astype(BF16)

    def give_back(p, o):
        mine = rows_at(p * PAIR + me * 16, 16)
        theirs = rows_at(p * PAIR + ((me + o) % NT) * 16, 16)
        return remote(rs.at[theirs], rr.at[mine], r_s.at[p, o], r_r.at[p, o], tok_dev(o))

    def send_back(p):
        row = iota((PAIR, 2 * BLK), 0)
        place = jnp.where(
            (iota((PAIR, 2 * BLK), 1) == packed_row(row)) & ((row & 7) < CAP), 1.0, 0.0
        ).astype(BF16)
        rs[p * PAIR : (p + 1) * PAIR] = dot(place, so[p]).astype(BF16)
        for o in range(1, NT):
            give_back(p, o).start()
        mine = rows_at(p * PAIR + me * 16, 16)
        rr[mine] = rs[mine]

    def merge():
        for o in range(1, NT):
            stat_copy(o).wait_recv()
            sum_copy(o).wait_recv()
        peak = st_r[0, 0:H]
        for j in range(1, NT):
            peak = jnp.maximum(peak, st_r[j, 0:H])
        total = jnp.zeros((H, ROWS), F32)
        for j in range(NT):
            total = total + st_r[j, H : 2 * H] * jnp.exp(st_r[j, 0:H] - peak)
        inverse = 1.0 / total
        acc[...] = jnp.zeros_like(acc)

        def add(j, _):
            share = st_r[j, H : 2 * H] * jnp.exp(st_r[j, 0:H] - peak) * inverse
            acc[...] += dot_t(share.astype(BF16), spread[...]) * nr[j].astype(F32)
            return 0

        lax.fori_loop(0, NT, add, 0)
        ow_copy.wait()
        acc[...] = dot(acc[...].astype(BF16), owb[...])

    def take_back(p):
        for o in range(1, NT):
            give_back(p, o).wait_recv()
        back = rr[p * PAIR : (p + 1) * PAIR]
        cols = pl.ds(p * PAIR, PAIR)
        acc[...] += dot(chi[:, cols], back) + dot(clo[:, cols], back)

    aggregate_range(1, 6)
    dispatch_arrived(0)
    compact(0)
    gather_first(0)
    gather_first(1)
    aggregate_range(6, 9)
    dispatch_arrived(1)
    compact(1)
    gather_second(0)
    gather_first(2)
    aggregate_range(9, 12)
    gather_second(1)
    gather_first(3)
    gather_third(0)
    experts_of(0)
    aggregate_range(12, 14)
    gather_second(2)
    sum_first(0)
    gather_third(1)
    experts_of(1)
    aggregate_range(14, 17)
    own_sum = pltpu.make_async_copy(ns.at[me], nr.at[me], own_sem.at[0])
    own_stat = pltpu.make_async_copy(st_s.at[me], st_r.at[me], own_sem.at[1])
    own_sum.start()
    own_stat.start()
    gather_second(3)
    sum_second(0)
    sum_first(1)
    gather_third(2)
    experts_of(2)
    sum_third(0)
    sum_second(1)
    sum_first(2)
    gather_third(3)
    experts_of(3)
    sum_third(1)
    send_back(0)
    sum_second(2)
    sum_first(3)
    own_sum.wait()
    own_stat.wait()
    merge()
    sum_second(3)
    sum_third(2)
    take_back(0)
    sum_third(3)
    send_back(1)
    take_back(1)
    out[...] = acc[...].astype(BF16)

    for p in range(2):
        for o in range(1, NT):
            dispatch(p, o).wait_send()
            give_back(p, o).wait_send()
    for o in range(1, NT):
        sum_copy(o).wait_send()
        stat_copy(o).wait_send()
    for e in range(GROUP):
        for kind in range(9):
            gather_copy(e, kind).wait_send()
        sibling_copy(e).wait_send()
        for kind in range(1, 7):
            sum_step(e, kind).wait_send()


def shards(
    x_var,
    var_ids,
    var_embed,
    score_vecs,
    v_weight,
    out_weight,
    second_half,
    norm_gain,
    routes,
    route_weights,
    w_gate,
    w_up,
    w_down,
):
    vmem = pl.BlockSpec(memory_space=pltpu.VMEM)
    anywhere = pl.BlockSpec(memory_space=pl.ANY)
    dma = pltpu.SemaphoreType.DMA
    return pl.pallas_call(
        kernel,
        out_shape=jax.ShapeDtypeStruct((ROWS, D), BF16),
        in_specs=[
            anywhere,
            vmem,
            vmem,
            vmem,
            anywhere,
            anywhere,
            vmem,
            vmem,
            vmem,
            vmem,
            anywhere,
            anywhere,
            anywhere,
        ],
        out_specs=vmem,
        scratch_shapes=[
            pltpu.VMEM((GROUP, D, 2 * FF), BF16),
            pltpu.VMEM((GROUP, FF, D), BF16),
            pltpu.VMEM((D, D), BF16),
            pltpu.VMEM((D, D), BF16),
            pltpu.VMEM((XSLOTS, VARS, ROWS, D), BF16),
            pltpu.VMEM((8, D), F32),
            pltpu.VMEM((H, D), BF16),
            pltpu.VMEM((H, D), BF16),
            pltpu.VMEM((ROWS, 2 * PAIR), BF16),
            pltpu.VMEM((ROWS, 2 * PAIR), BF16),
            pltpu.VMEM((2 * PAIR, D), BF16),
            pltpu.VMEM((2 * PAIR, D), BF16),
            pltpu.VMEM((GROUP, 2 * HALF, D), BF16),
            pltpu.VMEM((GROUP, 2 * HALF, D), BF16),
            pltpu.VMEM((GROUP, HALF, D), BF16),
            pltpu.VMEM((GROUP, 2, 64, D), BF16),
            pltpu.VMEM((GROUP, 2, BLK, D), BF16),
            pltpu.VMEM((2, 2 * BLK, D), BF16),
            pltpu.VMEM((2 * PAIR, D), BF16),
            pltpu.VMEM((2 * PAIR, D), BF16),
            pltpu.VMEM((NT, ROWS, D), BF16),
            pltpu.VMEM((NT, ROWS, D), BF16),
            pltpu.VMEM((NT, 2 * H, ROWS), F32),
            pltpu.VMEM((NT, 2 * H, ROWS), F32),
            pltpu.VMEM((ROWS, D), F32),
            dma((XSLOTS,)),
            dma((2 + 3 * GROUP,)),
            dma((2, NT)),
            dma((2, NT)),
            dma((GROUP, 9)),
            dma((GROUP, 9)),
            dma((GROUP, 7)),
            dma((GROUP, 7)),
            dma((2, NT)),
            dma((2, NT)),
            dma((NT,)),
            dma((NT,)),
            dma((NT,)),
            dma((NT,)),
            dma((2,)),
        ],
        compiler_params=pltpu.CompilerParams(
            collective_id=0, has_side_effects=True, vmem_limit_bytes=62 * 2**20
        ),
        cost_estimate=pl.CostEstimate(
            flops=20_000_000_000, bytes_accessed=24_000_000, transcendentals=1_000_000
        ),
    )(
        x_var,
        var_ids.reshape(VARS, 1),
        var_embed,
        score_vecs,
        v_weight,
        out_weight,
        second_half,
        norm_gain.reshape(1, D),
        routes,
        route_weights,
        w_gate,
        w_up,
        w_down,
    )


def solution(mesh):
    in_specs = (
        P("tok", None, "exp", None),
        P("tok"),
        P(),
        P(),
        P(),
        P(),
        P(("tok", "exp"), None),
        P(),
        P(("tok", "exp"), None),
        P(("tok", "exp"), None),
        P("tok", None, "exp"),
        P("tok", None, "exp"),
        P("tok", "exp", None),
    )
    out_specs = P(("tok", "exp"), None)
    return jax.shard_map(shards, mesh=mesh, in_specs=in_specs, out_specs=out_specs, check_vma=False)
```

```python
import jax
import jax.numpy as jnp
from jax import lax
from jax.experimental import pallas as pl
from jax.experimental.pallas import tpu as pltpu
from jax.sharding import PartitionSpec as P

MESH = pl.DeviceIdType.MESH
BF16 = jnp.bfloat16
F32 = jnp.float32
D = 1024
H = 16
VARS = 3
ROWS = 128
EXPERTS = 64
GROUP = 4
FF = 256
CAP = 7
NT = 16
NZ = 4
BLK = NT * CAP
HALF = NZ * BLK
WIDE = D // 2
HH = H // 2
MSG = NT * 16
XSLOTS = 3


def dot(a, b):
    return jnp.dot(a, b, preferred_element_type=F32)


def dot_t(a, b):
    return lax.dot_general(a, b, (((0,), (0,)), ((), ())), preferred_element_type=F32)


def iota(shape, dim):
    return lax.broadcasted_iota(jnp.int32, shape, dim)


def kernel(
    x,
    ids,
    embed,
    svec,
    vw,
    ow,
    half,
    gain,
    routes,
    rweights,
    wg,
    wu,
    wd,
    out,
    wgu,
    wdn,
    vwb,
    owb,
    xbuf,
    hbuf,
    lab,
    svp,
    spread,
    comb,
    pk,
    rb,
    ag,
    pt,
    sb,
    zr1,
    zr2,
    so,
    rs,
    rr,
    ns,
    n1r,
    n2s,
    n2r,
    st_s,
    st1r,
    st2s,
    st2r,
    acc,
    xsem,
    wsem,
    a_s,
    a_r,
    g_s,
    g_r,
    p_s,
    p_r,
    r_s,
    r_r,
    n1_s,
    n1_r,
    t1_s,
    t1_r,
    n2_s,
    n2_r,
    t2_s,
    t2_r,
):
    me = lax.axis_index("tok")
    ex = lax.axis_index("exp")
    z = ex // 2
    core = ex % 2
    y = me // 4
    xx = me % 4
    up = (me, ((z + 1) % NZ) * 2 + core)
    down = (me, ((z + NZ - 1) % NZ) * 2 + core)
    sib = (me, z * 2 + (1 - core))

    def tok_dev(o):
        return ((me + o) % NT, ex)

    def remote(src, dst, send, recv, dev):
        return pltpu.make_async_remote_copy(
            src_ref=src, dst_ref=dst, send_sem=send, recv_sem=recv, device_id=dev, device_id_type=MESH
        )

    def rows_at(start, size):
        return pl.ds(pl.multiple_of(start, 16), size)

    def along_x(dx):
        return (y * 4 + (xx + dx) % 4, ex)

    def along_y(dy):
        return (((y + dy) % 4) * 4 + xx, ex)

    def offsets(o):
        return (o + 1 + o // 4) % 4, (o + 1) % 4

    def x_copy(o):
        slot = o % XSLOTS
        dy, dx = offsets(o)
        dest = ((y + dy) % 4) * 4 + (xx + dx) % 4
        return pltpu.make_async_copy(x.at[:, dest], xbuf.at[slot], xsem.at[slot])

    vw_copy = pltpu.make_async_copy(vw, vwb, wsem.at[0])
    ow_copy = pltpu.make_async_copy(ow, owb, wsem.at[1])
    w_copies = []
    for e in range(GROUP):
        w_copies.append(
            (
                pltpu.make_async_copy(wg.at[e], wgu.at[e, :, 0:FF], wsem.at[2 + 3 * e]),
                pltpu.make_async_copy(wu.at[e], wgu.at[e, :, FF : 2 * FF], wsem.at[3 + 3 * e]),
                pltpu.make_async_copy(wd.at[e], wdn.at[e], wsem.at[4 + 3 * e]),
            )
        )

    half_copy = pltpu.make_async_copy(half, hbuf, wsem.at[2 + 3 * GROUP])
    half_copy.start()
    barrier = pltpu.get_barrier_semaphore()
    greeted = [tok_dev(o) for o in range(1, NT)] + [up, down, sib]
    for dev in greeted:
        pl.semaphore_signal(barrier, inc=1, device_id=dev, device_id_type=MESH)

    vw_copy.start()
    for o in range(XSLOTS):
        x_copy(o).start()
    for group in w_copies:
        for copy in group:
            copy.start()
    ow_copy.start()

    route0 = routes[0:1, :]
    route1 = routes[1:2, :]
    experts = iota((EXPERTS, ROWS), 0)
    named0 = route0 == experts
    named1 = route1 == experts
    either = jnp.where(named0 | named1, 1.0, 0.0).astype(BF16)
    before = jnp.where(iota((ROWS, ROWS), 0) < iota((ROWS, ROWS), 1), 1.0, 0.0).astype(BF16)
    count = dot(either, before)

    def target(route, named):
        slot = jnp.sum(jnp.where(named, count, 0.0), axis=0, keepdims=True).astype(jnp.int32)
        return route * 8 + slot

    target0 = target(route0, named0)
    target1 = target(route1, named1)
    half_copy.wait()
    level = hbuf[...].astype(F32)
    scale = lax.rsqrt(jnp.mean(level * level, axis=-1, keepdims=True) + 1e-06)
    normed = (level * scale * gain[...].astype(F32).reshape(1, D)).astype(BF16)
    msg_row = iota((MSG, ROWS), 0)
    msg_key = jnp.right_shift(msg_row, 4) * (GROUP * 8) + (msg_row & 7)
    second = (jnp.right_shift(iota((MSG, WIDE), 0), 3) & 1) == 1

    def halves(full):
        return jnp.where(second, full[:, WIDE:], full[:, :WIDE]).astype(BF16)

    def here(e):
        return msg_key == target0 - e * 8, msg_key == target1 - e * 8

    for e in range(GROUP):
        here0, here1 = here(e)
        placing = jnp.where(here0 | here1, 1.0, 0.0).astype(BF16)
        pk[e] = halves(dot(placing, normed))

    pl.semaphore_wait(barrier, len(greeted))

    def msg(i):
        return rows_at(i * 16, 16)

    def dispatch(e, o):
        there = (me + o) % NT
        return remote(pk.at[e, msg(there)], rb.at[e, msg(me)], a_s.at[e, o], a_r.at[e, o], tok_dev(o))

    for e in range(GROUP):
        for o in range(1, NT):
            dispatch(e, o).start()

    def dispatch_arrived(e):
        rb[e, msg(me)] = pk[e, msg(me)]
        for o in range(1, NT):
            dispatch(e, o).wait_recv()

    msg_half = jnp.right_shift(msg_row, 3) & 1
    for e in range(GROUP):
        here0, here1 = here(e)
        weights = jnp.where(here0, rweights[0:1, :], 0.0) + jnp.where(here1, rweights[1:2, :], 0.0)
        for side in range(2):
            turned = jnp.transpose(jnp.where(msg_half == side, weights, 0.0))
            high = turned.astype(BF16)
            comb[e, side, 0:ROWS] = high
            comb[e, side, ROWS : 2 * ROWS] = (turned - high.astype(F32)).astype(BF16)

    picks = jnp.where(ids[...] == iota((embed.shape[0], VARS), 0), 1.0, 0.0).astype(BF16)
    lab[0:VARS] = dot_t(picks, embed[...])
    turned_scores = jnp.concatenate([svec[...].astype(F32), jnp.zeros((128 - H, D), F32)], axis=0)
    svp[...] = jnp.transpose(turned_scores).astype(BF16)
    spread[...] = jnp.where(jnp.right_shift(iota((H, D), 1), 6) == iota((H, D), 0), 1.0, 0.0).astype(BF16)
    vw_copy.wait()

    def sum_one(side, dy, dx):
        k = dy * 4 + dx
        if side == 0:
            slot, dev = (dx - 1) * 4 + dy, along_x(dx)
        else:
            slot, dev = (dy - 1) * 4 + dx, along_y(dy)
        return (
            remote(ns.at[k, side], n1r.at[side, slot], n1_s.at[side, k], n1_r.at[side, k], dev),
            remote(st_s.at[k, side], st1r.at[side, slot], t1_s.at[side, k], t1_r.at[side, k], dev),
        )

    def sum_two(side, d):
        dev = along_y(d) if side == 0 else along_x(d)
        return (
            remote(n2s.at[side, d], n2r.at[side, d - 1], n2_s.at[side, d], n2_r.at[side, d], dev),
            remote(st2s.at[side, d], st2r.at[side, d - 1], t2_s.at[side, d], t2_r.at[side, d], dev),
        )

    def aggregate(o, _):
        dy, dx = offsets(o)
        k = dy * 4 + dx
        slot = o % XSLOTS
        x_copy(o).wait()
        embedded = jnp.concatenate(
            [(xbuf[slot, v].astype(F32) + lab[v : v + 1]).astype(BF16) for v in range(VARS)], axis=0
        )
        scores = dot(embedded, svp[...])
        parts = [jnp.transpose(scores[v * ROWS : (v + 1) * ROWS])[0:H] for v in range(VARS)]
        peak = jnp.maximum(jnp.maximum(parts[0], parts[1]), parts[2])
        expo = [jnp.exp(part - peak) for part in parts]
        denom = expo[0] + expo[1] + expo[2]
        inverse = 1.0 / denom
        for side in range(2):
            st_s[k, side, 0:HH] = peak[side * HH : (side + 1) * HH]
            st_s[k, side, HH : 2 * HH] = denom[side * HH : (side + 1) * HH]
        values = dot(embedded, vwb[...])
        mixed = None
        for v in range(VARS):
            share = dot_t((expo[v] * inverse).astype(BF16), spread[...])
            term = share * values[v * ROWS : (v + 1) * ROWS]
            mixed = term if mixed is None else mixed + term
        ns[k, 0] = mixed[:, :WIDE].astype(BF16)
        ns[k, 1] = mixed[:, WIDE:].astype(BF16)

        @pl.when(dx > 0)
        def _():
            for copy in sum_one(0, dy, dx):
                copy.start()

        @pl.when(dy > 0)
        def _():
            for copy in sum_one(1, dy, dx):
                copy.start()

        @pl.when(o + XSLOTS < NT)
        def _():
            x_copy(o + XSLOTS).start()

        return 0

    def aggregate_range(low, high_):
        lax.fori_loop(low, high_, aggregate, 0)

    mine_ag = (core * NZ + z) * BLK

    def packed_row(row):
        return jnp.where((row & 7) < CAP, jnp.right_shift(row, 4) * CAP + (row & 7), -1)

    def compact(e):
        col = iota((BLK, MSG), 1)
        match = iota((BLK, MSG), 0) == packed_row(col)
        for side in range(2):
            pick = jnp.where(match & ((jnp.right_shift(col, 3) & 1) == side), 1.0, 0.0).astype(BF16)
            ag[e, rows_at(mine_ag, BLK), side * WIDE : (side + 1) * WIDE] = dot(pick, rb[e]).astype(BF16)

    def low_rows(e):
        return 64 if e % 2 == 0 else 48

    def block_row(c, dz):
        return (c * NZ + (z + dz) % NZ) * BLK

    def gather_copy(e, kind):
        low = low_rows(e)
        start, size, dev = {
            0: (block_row(core, 0), BLK, up),
            1: (block_row(core, 0), BLK, down),
            2: (block_row(core, NZ - 1), low, up),
            3: (block_row(core, 1) + low, BLK - low, down),
            4: (block_row(core, 0), BLK, sib),
            5: (block_row(core, NZ - 1), BLK, sib),
            6: (block_row(core, 1), BLK, sib),
            7: (block_row(core, 2), low, sib),
            8: (block_row(core, 2) + low, BLK - low, sib),
        }[kind]
        place = ag.at[e, rows_at(start, size)]
        return remote(place, place, g_s.at[e, kind], g_r.at[e, kind], dev)

    def gather_recv(e, kind):
        low = low_rows(e)
        start, size, dev = {
            0: (block_row(core, NZ - 1), BLK, down),
            1: (block_row(core, 1), BLK, up),
            2: (block_row(core, 2), low, down),
            3: (block_row(core, 2) + low, BLK - low, up),
            4: (block_row(1 - core, 0), BLK, sib),
            5: (block_row(1 - core, NZ - 1), BLK, sib),
            6: (block_row(1 - core, 1), BLK, sib),
            7: (block_row(1 - core, 2), low, sib),
            8: (block_row(1 - core, 2) + low, BLK - low, sib),
        }[kind]
        place = ag.at[e, rows_at(start, size)]
        remote(place, place, g_s.at[e, kind], g_r.at[e, kind], dev).wait_recv()

    def gather_first(e):
        gather_copy(e, 0).start()
        gather_copy(e, 1).start()
        gather_copy(e, 4).start()

    def gather_second(e):
        gather_recv(e, 0)
        gather_copy(e, 2).start()
        gather_copy(e, 5).start()
        gather_recv(e, 1)
        gather_copy(e, 3).start()
        gather_copy(e, 6).start()

    def gather_third(e):
        gather_recv(e, 2)
        gather_copy(e, 7).start()
        gather_recv(e, 3)
        gather_copy(e, 8).start()

    def ffn(e, start):
        rows = rows_at(start, HALF)
        both = dot(ag[e, rows], wgu[e])
        gate = both[:, 0:FF]
        hidden = (gate / (1.0 + jnp.exp(-gate)) * both[:, FF : 2 * FF]).astype(BF16)
        pt[e, rows] = dot(hidden, wdn[e]).astype(BF16)

    def sibling_copy(e):
        return remote(
            pt.at[e, rows_at((1 - core) * HALF, HALF)], sb.at[e], p_s.at[e, 0], p_r.at[e, 0], sib
        )

    def experts_of(e):
        for copy in w_copies[e]:
            copy.wait()
        ffn(e, core * HALF)
        for kind in range(4, 9):
            gather_recv(e, kind)
        ffn(e, (1 - core) * HALF)
        sibling_copy(e).start()

    def part(e, dz, start, size):
        return pt.at[e, rows_at(block_row(core, dz) + start, size)]

    def sum_step(e, kind):
        low = low_rows(e)
        src, dst, dev = {
            1: (part(e, 2, 0, low), zr1.at[e, 0, 0:low], up),
            2: (part(e, 2, low, BLK - low), zr1.at[e, 1, 0 : BLK - low], down),
            3: (part(e, 1, low, BLK - low), zr2.at[e, 0, low:BLK], up),
            4: (part(e, 1, 0, low), zr2.at[e, 0, 0:low], up),
            5: (part(e, NZ - 1, 0, low), zr2.at[e, 1, 0:low], down),
            6: (part(e, NZ - 1, low, BLK - low), zr2.at[e, 1, low:BLK], down),
        }[kind]
        return remote(src, dst, p_s.at[e, kind], p_r.at[e, kind], dev)

    def add_sibling(e, dz):
        here = rows_at(block_row(core, dz), BLK)
        there = rows_at(((z + dz) % NZ) * BLK, BLK)
        pt[e, here] = (pt[e, here].astype(F32) + sb[e, there].astype(F32)).astype(BF16)

    def sum_first(e):
        sibling_copy(e).wait_recv()
        add_sibling(e, 2)
        sum_step(e, 1).start()
        sum_step(e, 2).start()
        add_sibling(e, 1)
        sum_step(e, 3).start()
        add_sibling(e, NZ - 1)
        sum_step(e, 5).start()
        add_sibling(e, 0)

    def sum_second(e):
        low = low_rows(e)
        sum_step(e, 1).wait_recv()
        here = rows_at(block_row(core, 1), low)
        pt[e, here] = (pt[e, here].astype(F32) + zr1[e, 0, 0:low].astype(F32)).astype(BF16)
        sum_step(e, 4).start()
        sum_step(e, 2).wait_recv()
        here = rows_at(block_row(core, NZ - 1) + low, BLK - low)
        pt[e, here] = (pt[e, here].astype(F32) + zr1[e, 1, 0 : BLK - low].astype(F32)).astype(BF16)
        sum_step(e, 6).start()

    def sum_third(e):
        for kind in range(3, 7):
            sum_step(e, kind).wait_recv()
        here = rows_at(block_row(core, 0), BLK)
        total = pt[e, here].astype(F32) + zr2[e, 0].astype(F32) + zr2[e, 1].astype(F32)
        so[...] = total.astype(BF16)
        send_back(e)

    def give_back(e, o):
        there = (me + o) % NT
        return remote(rs.at[e, msg(there)], rr.at[e, msg(me)], r_s.at[e, o], r_r.at[e, o], tok_dev(o))

    def send_back(e):
        place = jnp.where(
            iota((MSG, BLK), 1) == packed_row(iota((MSG, BLK), 0)), 1.0, 0.0
        ).astype(BF16)
        rs[e] = halves(dot(place, so[...]))
        for o in range(1, NT):
            give_back(e, o).start()
        rr[e, msg(me)] = rs[e, msg(me)]

    def merged(stats, sums):
        peak = stats[0][0:HH]
        for stat in stats[1:]:
            peak = jnp.maximum(peak, stat[0:HH])
        shares = [stat[HH : 2 * HH] * jnp.exp(stat[0:HH] - peak) for stat in stats]
        total = shares[0] + shares[1] + shares[2] + shares[3]
        inverse = 1.0 / total
        value = None
        for share, term in zip(shares, sums):
            wide = dot_t((share * inverse).astype(BF16), spread[0:HH, 0:WIDE])
            piece = wide * term.astype(F32)
            value = piece if value is None else value + piece
        return peak, total, value

    def merge_one(side, d):
        stats, sums = [], []
        k = d * 4 if side == 0 else d
        stats.append(st_s[k, side])
        sums.append(ns[k, side])
        for first in range(1, 4):
            dy, dx = (d, first) if side == 0 else (first, d)
            for copy in sum_one(side, dy, dx):
                copy.wait_recv()
            stats.append(st1r[side, (first - 1) * 4 + d])
            sums.append(n1r[side, (first - 1) * 4 + d])
        peak, total, value = merged(stats, sums)
        st2s[side, d, 0:HH] = peak
        st2s[side, d, HH : 2 * HH] = total
        n2s[side, d] = value.astype(BF16)
        if d > 0:
            for copy in sum_two(side, d):
                copy.start()

    def merge_two():
        for side in range(2):
            stats, sums = [st2s[side, 0]], [n2s[side, 0]]
            for d in range(1, 4):
                for copy in sum_two(side, d):
                    copy.wait_recv()
                stats.append(st2r[side, d - 1])
                sums.append(n2r[side, d - 1])
            acc[:, side * WIDE : (side + 1) * WIDE] = merged(stats, sums)[2]
        ow_copy.wait()
        acc[...] = dot(acc[...].astype(BF16), owb[...])

    def take_back(e):
        for o in range(1, NT):
            give_back(e, o).wait_recv()
        for side in range(2):
            both = dot(comb[e, side], rr[e])
            acc[:, side * WIDE : (side + 1) * WIDE] += both[0:ROWS] + both[ROWS : 2 * ROWS]

    aggregate_range(0, 3)
    dispatch_arrived(0)
    compact(0)
    gather_first(0)
    dispatch_arrived(1)
    compact(1)
    gather_first(1)
    aggregate_range(3, 6)
    dispatch_arrived(2)
    compact(2)
    gather_second(0)
    gather_first(2)
    aggregate_range(6, 9)
    dispatch_arrived(3)
    compact(3)
    gather_second(1)
    gather_first(3)
    gather_third(0)
    aggregate_range(9, 10)
    experts_of(0)
    aggregate_range(10, 12)
    gather_second(2)
    sum_first(0)
    gather_third(1)
    experts_of(1)
    aggregate_range(12, 14)
    gather_second(3)
    sum_second(0)
    sum_first(1)
    gather_third(2)
    experts_of(2)
    aggregate_range(14, 16)
    sum_third(0)
    sum_second(1)
    sum_first(2)
    gather_third(3)
    experts_of(3)
    for d in range(1, 4):
        merge_one(0, d)
        merge_one(1, d)
    sum_third(1)
    sum_second(2)
    sum_first(3)
    merge_one(0, 0)
    merge_one(1, 0)
    sum_third(2)
    sum_second(3)
    merge_two()
    take_back(0)
    take_back(1)
    sum_third(3)
    take_back(2)
    take_back(3)
    out[...] = acc[...].astype(BF16)

    for e in range(GROUP):
        for o in range(1, NT):
            dispatch(e, o).wait_send()
            give_back(e, o).wait_send()
        for kind in range(9):
            gather_copy(e, kind).wait_send()
        sibling_copy(e).wait_send()
        for kind in range(1, 7):
            sum_step(e, kind).wait_send()
    for d in range(4):
        for first in range(1, 4):
            for copy in sum_one(0, d, first) + sum_one(1, first, d):
                copy.wait_send()
        if d > 0:
            for copy in sum_two(0, d) + sum_two(1, d):
                copy.wait_send()


def shards(
    x_var,
    var_ids,
    var_embed,
    score_vecs,
    v_weight,
    out_weight,
    second_half,
    norm_gain,
    routes,
    route_weights,
    w_gate,
    w_up,
    w_down,
):
    vmem = pl.BlockSpec(memory_space=pltpu.VMEM)
    anywhere = pl.BlockSpec(memory_space=pl.ANY)
    dma = pltpu.SemaphoreType.DMA
    return pl.pallas_call(
        kernel,
        out_shape=jax.ShapeDtypeStruct((ROWS, D), BF16),
        in_specs=[
            anywhere,
            vmem,
            vmem,
            vmem,
            anywhere,
            anywhere,
            anywhere,
            vmem,
            vmem,
            vmem,
            anywhere,
            anywhere,
            anywhere,
        ],
        out_specs=vmem,
        scratch_shapes=[
            pltpu.VMEM((GROUP, D, 2 * FF), BF16),
            pltpu.VMEM((GROUP, FF, D), BF16),
            pltpu.VMEM((D, D), BF16),
            pltpu.VMEM((D, D), BF16),
            pltpu.VMEM((XSLOTS, VARS, ROWS, D), BF16),
            pltpu.VMEM((ROWS, D), BF16),
            pltpu.VMEM((8, D), F32),
            pltpu.VMEM((D, 128), BF16),
            pltpu.VMEM((H, D), BF16),
            pltpu.VMEM((GROUP, 2, 2 * ROWS, MSG), BF16),
            pltpu.VMEM((GROUP, MSG, WIDE), BF16),
            pltpu.VMEM((GROUP, MSG, WIDE), BF16),
            pltpu.VMEM((GROUP, 2 * HALF, D), BF16),
            pltpu.VMEM((GROUP, 2 * HALF, D), BF16),
            pltpu.VMEM((GROUP, HALF, D), BF16),
            pltpu.VMEM((GROUP, 2, 64, D), BF16),
            pltpu.VMEM((GROUP, 2, BLK, D), BF16),
            pltpu.VMEM((BLK, D), BF16),
            pltpu.VMEM((GROUP, MSG, WIDE), BF16),
            pltpu.VMEM((GROUP, MSG, WIDE), BF16),
            pltpu.VMEM((NT, 2, ROWS, WIDE), BF16),
            pltpu.VMEM((2, 12, ROWS, WIDE), BF16),
            pltpu.VMEM((2, 4, ROWS, WIDE), BF16),
            pltpu.VMEM((2, 3, ROWS, WIDE), BF16),
            pltpu.VMEM((NT, 2, H, ROWS), F32),
            pltpu.VMEM((2, 12, H, ROWS), F32),
            pltpu.VMEM((2, 4, H, ROWS), F32),
            pltpu.VMEM((2, 3, H, ROWS), F32),
            pltpu.VMEM((ROWS, D), F32),
            dma((XSLOTS,)),
            dma((3 + 3 * GROUP,)),
            dma((GROUP, NT)),
            dma((GROUP, NT)),
            dma((GROUP, 9)),
            dma((GROUP, 9)),
            dma((GROUP, 7)),
            dma((GROUP, 7)),
            dma((GROUP, NT)),
            dma((GROUP, NT)),
            dma((2, NT)),
            dma((2, NT)),
            dma((2, NT)),
            dma((2, NT)),
            dma((2, 4)),
            dma((2, 4)),
            dma((2, 4)),
            dma((2, 4)),
        ],
        compiler_params=pltpu.CompilerParams(
            collective_id=0, has_side_effects=True, vmem_limit_bytes=62 * 2**20
        ),
        cost_estimate=pl.CostEstimate(
            flops=20_000_000_000, bytes_accessed=24_000_000, transcendentals=1_000_000
        ),
    )(
        x_var,
        var_ids.reshape(1, VARS),
        var_embed,
        score_vecs.T,
        v_weight,
        out_weight,
        second_half,
        norm_gain,
        routes.T,
        route_weights.T,
        w_gate,
        w_up,
        w_down,
    )


def solution(mesh):
    in_specs = (
        P("tok", None, "exp", None),
        P("tok"),
        P(),
        P(),
        P(),
        P(),
        P(("tok", "exp"), None),
        P(),
        P(("tok", "exp"), None),
        P(("tok", "exp"), None),
        P("tok", None, "exp"),
        P("tok", None, "exp"),
        P("tok", "exp", None),
    )
    out_specs = P(("tok", "exp"), None)
    return jax.shard_map(shards, mesh=mesh, in_specs=in_specs, out_specs=out_specs, check_vma=False)
```

```python
import jax
import jax.numpy as jnp
from jax import lax
from jax.experimental import pallas as pl
from jax.experimental.pallas import tpu as pltpu
from jax.sharding import PartitionSpec as P

MESH = pl.DeviceIdType.MESH
BF16 = jnp.bfloat16
F32 = jnp.float32
D = 1024
H = 16
VARS = 3
ROWS = 128
EXPERTS = 64
GROUP = 4
FF = 256
CAP = 7
NT = 16
NZ = 4
BLK = NT * CAP
HALF = NZ * BLK
WIDE = D // 2
HH = H // 2
MSG = NT * 16
MSG_SENT = MSG - 16
XSLOTS = 3


def dot(a, b):
    return jnp.dot(a, b, preferred_element_type=F32)


def dot_t(a, b):
    return lax.dot_general(a, b, (((0,), (0,)), ((), ())), preferred_element_type=F32)


def iota(shape, dim):
    return lax.broadcasted_iota(jnp.int32, shape, dim)


def kernel(
    x,
    ids,
    embed,
    svec,
    vw,
    ow,
    half,
    gain,
    routes,
    rweights,
    wg,
    wu,
    wd,
    out,
    wgu,
    wdn,
    vwb,
    owb,
    xbuf,
    hbuf,
    lab,
    svp,
    spread,
    comb,
    pk,
    rb,
    ag,
    pt,
    sb,
    zr1,
    zr2,
    so,
    rs,
    rr,
    ns,
    n1r,
    n2s,
    n2r,
    st_s,
    st1r,
    st2s,
    st2r,
    acc,
    xsem,
    wsem,
    a_s,
    a_r,
    g_s,
    g_r,
    p_s,
    p_r,
    r_s,
    r_r,
    n1_s,
    n1_r,
    t1_s,
    t1_r,
    n2_s,
    n2_r,
    t2_s,
    t2_r,
):
    me = lax.axis_index("tok")
    ex = lax.axis_index("exp")
    z = ex // 2
    core = ex % 2
    y = me // 4
    xx = me % 4
    up = (me, ((z + 1) % NZ) * 2 + core)
    down = (me, ((z + NZ - 1) % NZ) * 2 + core)
    sib = (me, z * 2 + (1 - core))

    def tok_dev(o):
        return ((me + o) % NT, ex)

    def remote(src, dst, send, recv, dev):
        return pltpu.make_async_remote_copy(
            src_ref=src, dst_ref=dst, send_sem=send, recv_sem=recv, device_id=dev, device_id_type=MESH
        )

    def rows_at(start, size):
        return pl.ds(pl.multiple_of(start, 16), size)

    def along_x(dx):
        return (y * 4 + (xx + dx) % 4, ex)

    def along_y(dy):
        return (((y + dy) % 4) * 4 + xx, ex)

    def offsets(o):
        return (o + 1 + o // 4) % 4, (o + 1) % 4

    def x_copy(o):
        slot = o % XSLOTS
        dy, dx = offsets(o)
        dest = ((y + dy) % 4) * 4 + (xx + dx) % 4
        return pltpu.make_async_copy(x.at[:, dest], xbuf.at[slot], xsem.at[slot])

    vw_copy = pltpu.make_async_copy(vw, vwb, wsem.at[0])
    ow_copy = pltpu.make_async_copy(ow, owb, wsem.at[1])
    w_copies = []
    for e in range(GROUP):
        w_copies.append(
            (
                pltpu.make_async_copy(wg.at[e], wgu.at[e, :, 0:FF], wsem.at[2 + 3 * e]),
                pltpu.make_async_copy(wu.at[e], wgu.at[e, :, FF : 2 * FF], wsem.at[3 + 3 * e]),
                pltpu.make_async_copy(wd.at[e], wdn.at[e], wsem.at[4 + 3 * e]),
            )
        )

    half_copy = pltpu.make_async_copy(half, hbuf, wsem.at[2 + 3 * GROUP])
    half_copy.start()
    barrier = pltpu.get_barrier_semaphore()
    greeted = [tok_dev(o) for o in range(1, NT)] + [up, down, sib]
    for dev in greeted:
        pl.semaphore_signal(barrier, inc=1, device_id=dev, device_id_type=MESH)

    vw_copy.start()
    for o in range(XSLOTS):
        x_copy(o).start()
    for group in w_copies:
        for copy in group:
            copy.start()
    ow_copy.start()

    route0 = routes[0:1, :]
    route1 = routes[1:2, :]
    experts = iota((EXPERTS, ROWS), 0)
    named0 = route0 == experts
    named1 = route1 == experts
    either = jnp.where(named0 | named1, 1.0, 0.0).astype(BF16)
    before = jnp.where(iota((ROWS, ROWS), 0) < iota((ROWS, ROWS), 1), 1.0, 0.0).astype(BF16)
    count = dot(either, before)

    def target(route, named):
        slot = jnp.sum(jnp.where(named, count, 0.0), axis=0, keepdims=True).astype(jnp.int32)
        return route * 8 + slot

    target0 = target(route0, named0)
    target1 = target(route1, named1)
    half_copy.wait()
    level = hbuf[...].astype(F32)
    scale = lax.rsqrt(jnp.mean(level * level, axis=-1, keepdims=True) + 1e-06)
    normed = (level * scale * gain[...].astype(F32).reshape(1, D)).astype(BF16)
    msg_row = iota((MSG, ROWS), 0)
    msg_key = jnp.right_shift(msg_row, 4) * (GROUP * 8) + (msg_row & 7)
    second = (jnp.right_shift(iota((MSG, WIDE), 0), 3) & 1) == 1

    def halves(full):
        return jnp.where(second, full[:, WIDE:], full[:, :WIDE]).astype(BF16)

    def here(e):
        return msg_key == target0 - e * 8, msg_key == target1 - e * 8

    for e in range(GROUP):
        here0, here1 = here(e)
        placing = jnp.where(here0 | here1, 1.0, 0.0).astype(BF16)
        pk[e] = halves(dot(placing, normed))

    pl.semaphore_wait(barrier, len(greeted))

    def landed(place, sem):
        pltpu.make_async_copy(place, place, sem).wait()

    def msg(i):
        return rows_at(i * 16, 16)

    def dispatch(e, o):
        there = (me + o) % NT
        return remote(pk.at[e, msg(there)], rb.at[e, msg(me)], a_s.at[e], a_r.at[e], tok_dev(o))

    for e in range(GROUP):
        for o in range(1, NT):
            dispatch(e, o).start()

    def dispatch_arrived(e):
        landed(rb.at[e, 0:MSG_SENT], a_r.at[e])
        rb[e, msg(me)] = pk[e, msg(me)]

    msg_half = jnp.right_shift(msg_row, 3) & 1
    for e in range(GROUP):
        here0, here1 = here(e)
        weights = jnp.where(here0, rweights[0:1, :], 0.0) + jnp.where(here1, rweights[1:2, :], 0.0)
        for side in range(2):
            turned = jnp.transpose(jnp.where(msg_half == side, weights, 0.0))
            high = turned.astype(BF16)
            comb[e, side, 0:ROWS] = high
            comb[e, side, ROWS : 2 * ROWS] = (turned - high.astype(F32)).astype(BF16)

    picks = jnp.where(ids[...] == iota((embed.shape[0], VARS), 0), 1.0, 0.0).astype(BF16)
    lab[0:VARS] = dot_t(picks, embed[...])
    turned_scores = jnp.concatenate([svec[...].astype(F32), jnp.zeros((128 - H, D), F32)], axis=0)
    svp[...] = jnp.transpose(turned_scores).astype(BF16)
    spread[...] = jnp.where(jnp.right_shift(iota((H, D), 1), 6) == iota((H, D), 0), 1.0, 0.0).astype(BF16)
    vw_copy.wait()

    def sum_one(side, dy, dx):
        k = dy * 4 + dx
        if side == 0:
            d, first, dev = dy, dx - 1, along_x(dx)
        else:
            d, first, dev = dx, dy - 1, along_y(dy)
        return (
            remote(ns.at[k, side], n1r.at[side, d, first], n1_s.at[side], n1_r.at[side, d], dev),
            remote(st_s.at[k, side], st1r.at[side, d, first], t1_s.at[side], t1_r.at[side, d], dev),
        )

    def sum_two(side, d):
        dev = along_y(d) if side == 0 else along_x(d)
        return (
            remote(n2s.at[side, d], n2r.at[side, d - 1], n2_s.at[side], n2_r.at[side], dev),
            remote(st2s.at[side, d], st2r.at[side, d - 1], t2_s.at[side], t2_r.at[side], dev),
        )

    def aggregate(o, _):
        dy, dx = offsets(o)
        k = dy * 4 + dx
        slot = o % XSLOTS
        x_copy(o).wait()
        embedded = jnp.concatenate(
            [(xbuf[slot, v].astype(F32) + lab[v : v + 1]).astype(BF16) for v in range(VARS)], axis=0
        )
        scores = dot(embedded, svp[...])
        parts = [jnp.transpose(scores[v * ROWS : (v + 1) * ROWS])[0:H] for v in range(VARS)]
        peak = jnp.maximum(jnp.maximum(parts[0], parts[1]), parts[2])
        expo = [jnp.exp(part - peak) for part in parts]
        denom = expo[0] + expo[1] + expo[2]
        inverse = 1.0 / denom
        for side in range(2):
            st_s[k, side, 0:HH] = peak[side * HH : (side + 1) * HH]
            st_s[k, side, HH : 2 * HH] = denom[side * HH : (side + 1) * HH]
        values = dot(embedded, vwb[...])
        mixed = None
        for v in range(VARS):
            share = dot_t((expo[v] * inverse).astype(BF16), spread[...])
            term = share * values[v * ROWS : (v + 1) * ROWS]
            mixed = term if mixed is None else mixed + term
        ns[k, 0] = mixed[:, :WIDE].astype(BF16)
        ns[k, 1] = mixed[:, WIDE:].astype(BF16)

        @pl.when(dx > 0)
        def _():
            for copy in sum_one(0, dy, dx):
                copy.start()

        @pl.when(dy > 0)
        def _():
            for copy in sum_one(1, dy, dx):
                copy.start()

        @pl.when(o + XSLOTS < NT)
        def _():
            x_copy(o + XSLOTS).start()

        return 0

    def aggregate_range(low, high_):
        lax.fori_loop(low, high_, aggregate, 0)

    mine_ag = (core * NZ + z) * BLK

    def packed_row(row):
        return jnp.where((row & 7) < CAP, jnp.right_shift(row, 4) * CAP + (row & 7), -1)

    def compact(e):
        col = iota((BLK, MSG), 1)
        match = iota((BLK, MSG), 0) == packed_row(col)
        for side in range(2):
            pick = jnp.where(match & ((jnp.right_shift(col, 3) & 1) == side), 1.0, 0.0).astype(BF16)
            ag[e, rows_at(mine_ag, BLK), side * WIDE : (side + 1) * WIDE] = dot(pick, rb[e]).astype(BF16)

    def low_rows(e):
        return 64 if e % 2 == 0 else 48

    def block_row(c, dz):
        return (c * NZ + (z + dz) % NZ) * BLK

    def gather_copy(e, kind):
        low = low_rows(e)
        start, size, dev = {
            0: (block_row(core, 0), BLK, up),
            1: (block_row(core, 0), BLK, down),
            2: (block_row(core, NZ - 1), low, up),
            3: (block_row(core, 1) + low, BLK - low, down),
            4: (block_row(core, 0), BLK, sib),
            5: (block_row(core, NZ - 1), BLK, sib),
            6: (block_row(core, 1), BLK, sib),
            7: (block_row(core, 2), low, sib),
            8: (block_row(core, 2) + low, BLK - low, sib),
        }[kind]
        place = ag.at[e, rows_at(start, size)]
        return remote(place, place, g_s.at[e], g_r.at[e, min(kind, 4)], dev)

    def gather_recv(e, kind):
        low = low_rows(e)
        start, size = {
            0: (block_row(core, NZ - 1), BLK),
            1: (block_row(core, 1), BLK),
            2: (block_row(core, 2), low),
            3: (block_row(core, 2) + low, BLK - low),
            4: ((1 - core) * HALF, HALF),
        }[kind]
        landed(ag.at[e, rows_at(start, size)], g_r.at[e, kind])

    def gather_first(e):
        gather_copy(e, 0).start()
        gather_copy(e, 1).start()
        gather_copy(e, 4).start()

    def gather_second(e):
        gather_recv(e, 0)
        gather_copy(e, 2).start()
        gather_copy(e, 5).start()
        gather_recv(e, 1)
        gather_copy(e, 3).start()
        gather_copy(e, 6).start()

    def gather_third(e):
        gather_recv(e, 2)
        gather_copy(e, 7).start()
        gather_recv(e, 3)
        gather_copy(e, 8).start()

    def ffn(e, start):
        rows = rows_at(start, HALF)
        both = dot(ag[e, rows], wgu[e])
        gate = both[:, 0:FF]
        hidden = (gate / (1.0 + jnp.exp(-gate)) * both[:, FF : 2 * FF]).astype(BF16)
        pt[e, rows] = dot(hidden, wdn[e]).astype(BF16)

    def sibling_copy(e):
        return remote(
            pt.at[e, rows_at((1 - core) * HALF, HALF)], sb.at[e], p_s.at[e], p_r.at[e, 0], sib
        )

    def experts_of(e):
        for copy in w_copies[e]:
            copy.wait()
        ffn(e, core * HALF)
        gather_recv(e, 4)
        ffn(e, (1 - core) * HALF)
        sibling_copy(e).start()

    def part(e, dz, start, size):
        return pt.at[e, rows_at(block_row(core, dz) + start, size)]

    def sum_step(e, kind):
        low = low_rows(e)
        src, dst, dev = {
            1: (part(e, 2, 0, low), zr1.at[e, 0, 0:low], up),
            2: (part(e, 2, low, BLK - low), zr1.at[e, 1, 0 : BLK - low], down),
            3: (part(e, 1, low, BLK - low), zr2.at[e, 0, low:BLK], up),
            4: (part(e, 1, 0, low), zr2.at[e, 0, 0:low], up),
            5: (part(e, NZ - 1, 0, low), zr2.at[e, 1, 0:low], down),
            6: (part(e, NZ - 1, low, BLK - low), zr2.at[e, 1, low:BLK], down),
        }[kind]
        return remote(src, dst, p_s.at[e], p_r.at[e, min(kind, 3)], dev)

    def add_sibling(e, dz):
        here = rows_at(block_row(core, dz), BLK)
        there = rows_at(((z + dz) % NZ) * BLK, BLK)
        pt[e, here] = (pt[e, here].astype(F32) + sb[e, there].astype(F32)).astype(BF16)

    def sum_first(e):
        landed(sb.at[e], p_r.at[e, 0])
        add_sibling(e, 2)
        sum_step(e, 1).start()
        sum_step(e, 2).start()
        add_sibling(e, 1)
        sum_step(e, 3).start()
        add_sibling(e, NZ - 1)
        sum_step(e, 5).start()
        add_sibling(e, 0)

    def sum_second(e):
        low = low_rows(e)
        landed(zr1.at[e, 0, 0:low], p_r.at[e, 1])
        here = rows_at(block_row(core, 1), low)
        pt[e, here] = (pt[e, here].astype(F32) + zr1[e, 0, 0:low].astype(F32)).astype(BF16)
        sum_step(e, 4).start()
        landed(zr1.at[e, 1, 0 : BLK - low], p_r.at[e, 2])
        here = rows_at(block_row(core, NZ - 1) + low, BLK - low)
        pt[e, here] = (pt[e, here].astype(F32) + zr1[e, 1, 0 : BLK - low].astype(F32)).astype(BF16)
        sum_step(e, 6).start()

    def sum_third(e):
        landed(zr2.at[e], p_r.at[e, 3])
        here = rows_at(block_row(core, 0), BLK)
        total = pt[e, here].astype(F32) + zr2[e, 0].astype(F32) + zr2[e, 1].astype(F32)
        so[...] = total.astype(BF16)
        send_back(e)

    def give_back(e, o):
        there = (me + o) % NT
        return remote(rs.at[e, msg(there)], rr.at[e, msg(me)], r_s.at[e], r_r.at[e], tok_dev(o))

    def send_back(e):
        place = jnp.where(
            iota((MSG, BLK), 1) == packed_row(iota((MSG, BLK), 0)), 1.0, 0.0
        ).astype(BF16)
        rs[e] = halves(dot(place, so[...]))
        for o in range(1, NT):
            give_back(e, o).start()

    def merged(stats, sums):
        peak = stats[0][0:HH]
        for stat in stats[1:]:
            peak = jnp.maximum(peak, stat[0:HH])
        shares = [stat[HH : 2 * HH] * jnp.exp(stat[0:HH] - peak) for stat in stats]
        total = shares[0] + shares[1] + shares[2] + shares[3]
        inverse = 1.0 / total
        value = None
        for share, term in zip(shares, sums):
            wide = dot_t((share * inverse).astype(BF16), spread[0:HH, 0:WIDE])
            piece = wide * term.astype(F32)
            value = piece if value is None else value + piece
        return peak, total, value

    def merge_one(side, d):
        stats, sums = [], []
        k = d * 4 if side == 0 else d
        stats.append(st_s[k, side])
        sums.append(ns[k, side])
        landed(st1r.at[side, d], t1_r.at[side, d])
        landed(n1r.at[side, d], n1_r.at[side, d])
        for first in range(3):
            stats.append(st1r[side, d, first])
            sums.append(n1r[side, d, first])
        peak, total, value = merged(stats, sums)
        st2s[side, d, 0:HH] = peak
        st2s[side, d, HH : 2 * HH] = total
        n2s[side, d] = value.astype(BF16)
        if d > 0:
            for copy in sum_two(side, d):
                copy.start()

    def merge_two():
        for side in range(2):
            stats, sums = [st2s[side, 0]], [n2s[side, 0]]
            landed(st2r.at[side], t2_r.at[side])
            landed(n2r.at[side], n2_r.at[side])
            for d in range(1, 4):
                stats.append(st2r[side, d - 1])
                sums.append(n2r[side, d - 1])
            acc[:, side * WIDE : (side + 1) * WIDE] = merged(stats, sums)[2]
        ow_copy.wait()
        acc[...] = dot(acc[...].astype(BF16), owb[...])

    def take_back(e):
        landed(rr.at[e, 0:MSG_SENT], r_r.at[e])
        rr[e, msg(me)] = rs[e, msg(me)]
        for side in range(2):
            both = dot(comb[e, side], rr[e])
            acc[:, side * WIDE : (side + 1) * WIDE] += both[0:ROWS] + both[ROWS : 2 * ROWS]

    aggregate_range(0, 3)
    dispatch_arrived(0)
    compact(0)
    gather_first(0)
    dispatch_arrived(1)
    compact(1)
    gather_first(1)
    aggregate_range(3, 6)
    dispatch_arrived(2)
    compact(2)
    gather_second(0)
    gather_first(2)
    aggregate_range(6, 9)
    dispatch_arrived(3)
    compact(3)
    gather_second(1)
    gather_first(3)
    gather_third(0)
    aggregate_range(9, 10)
    experts_of(0)
    aggregate_range(10, 12)
    gather_second(2)
    sum_first(0)
    gather_third(1)
    experts_of(1)
    aggregate_range(12, 14)
    gather_second(3)
    sum_second(0)
    sum_first(1)
    gather_third(2)
    experts_of(2)
    aggregate_range(14, 16)
    sum_third(0)
    sum_second(1)
    sum_first(2)
    gather_third(3)
    experts_of(3)
    for d in range(1, 4):
        merge_one(0, d)
        merge_one(1, d)
    sum_third(1)
    sum_second(2)
    sum_first(3)
    merge_one(0, 0)
    merge_one(1, 0)
    sum_third(2)
    sum_second(3)
    merge_two()
    take_back(0)
    take_back(1)
    sum_third(3)
    take_back(2)
    take_back(3)
    out[...] = acc[...].astype(BF16)

    for e in range(GROUP):
        landed(pk.at[e, 0:MSG_SENT], a_s.at[e])
        landed(rs.at[e, 0:MSG_SENT], r_s.at[e])
        landed(ag.at[e, 0 : 7 * BLK], g_s.at[e])
        landed(pt.at[e, 0 : 7 * BLK], p_s.at[e])
    for side in range(2):
        landed(n1r.at[side], n1_s.at[side])
        landed(st1r.at[side], t1_s.at[side])
        landed(n2r.at[side], n2_s.at[side])
        landed(st2r.at[side], t2_s.at[side])


def shards(
    x_var,
    var_ids,
    var_embed,
    score_vecs,
    v_weight,
    out_weight,
    second_half,
    norm_gain,
    routes,
    route_weights,
    w_gate,
    w_up,
    w_down,
):
    vmem = pl.BlockSpec(memory_space=pltpu.VMEM)
    anywhere = pl.BlockSpec(memory_space=pl.ANY)
    dma = pltpu.SemaphoreType.DMA
    return pl.pallas_call(
        kernel,
        out_shape=jax.ShapeDtypeStruct((ROWS, D), BF16),
        in_specs=[
            anywhere,
            vmem,
            vmem,
            vmem,
            anywhere,
            anywhere,
            anywhere,
            vmem,
            vmem,
            vmem,
            anywhere,
            anywhere,
            anywhere,
        ],
        out_specs=vmem,
        scratch_shapes=[
            pltpu.VMEM((GROUP, D, 2 * FF), BF16),
            pltpu.VMEM((GROUP, FF, D), BF16),
            pltpu.VMEM((D, D), BF16),
            pltpu.VMEM((D, D), BF16),
            pltpu.VMEM((XSLOTS, VARS, ROWS, D), BF16),
            pltpu.VMEM((ROWS, D), BF16),
            pltpu.VMEM((8, D), F32),
            pltpu.VMEM((D, 128), BF16),
            pltpu.VMEM((H, D), BF16),
            pltpu.VMEM((GROUP, 2, 2 * ROWS, MSG), BF16),
            pltpu.VMEM((GROUP, MSG, WIDE), BF16),
            pltpu.VMEM((GROUP, MSG, WIDE), BF16),
            pltpu.VMEM((GROUP, 2 * HALF, D), BF16),
            pltpu.VMEM((GROUP, 2 * HALF, D), BF16),
            pltpu.VMEM((GROUP, HALF, D), BF16),
            pltpu.VMEM((GROUP, 2, 64, D), BF16),
            pltpu.VMEM((GROUP, 2, BLK, D), BF16),
            pltpu.VMEM((BLK, D), BF16),
            pltpu.VMEM((GROUP, MSG, WIDE), BF16),
            pltpu.VMEM((GROUP, MSG, WIDE), BF16),
            pltpu.VMEM((NT, 2, ROWS, WIDE), BF16),
            pltpu.VMEM((2, 4, 3, ROWS, WIDE), BF16),
            pltpu.VMEM((2, 4, ROWS, WIDE), BF16),
            pltpu.VMEM((2, 3, ROWS, WIDE), BF16),
            pltpu.VMEM((NT, 2, H, ROWS), F32),
            pltpu.VMEM((2, 4, 3, H, ROWS), F32),
            pltpu.VMEM((2, 4, H, ROWS), F32),
            pltpu.VMEM((2, 3, H, ROWS), F32),
            pltpu.VMEM((ROWS, D), F32),
            dma((XSLOTS,)),
            dma((3 + 3 * GROUP,)),
            dma((GROUP,)),
            dma((GROUP,)),
            dma((GROUP,)),
            dma((GROUP, 5)),
            dma((GROUP,)),
            dma((GROUP, 4)),
            dma((GROUP,)),
            dma((GROUP,)),
            dma((2,)),
            dma((2, 4)),
            dma((2,)),
            dma((2, 4)),
            dma((2,)),
            dma((2,)),
            dma((2,)),
            dma((2,)),
        ],
        compiler_params=pltpu.CompilerParams(
            collective_id=0, has_side_effects=True, vmem_limit_bytes=62 * 2**20
        ),
        cost_estimate=pl.CostEstimate(
            flops=20_000_000_000, bytes_accessed=24_000_000, transcendentals=1_000_000
        ),
    )(
        x_var,
        var_ids.reshape(1, VARS),
        var_embed,
        score_vecs.T,
        v_weight,
        out_weight,
        second_half,
        norm_gain,
        routes.T,
        route_weights.T,
        w_gate,
        w_up,
        w_down,
    )


def solution(mesh):
    in_specs = (
        P("tok", None, "exp", None),
        P("tok"),
        P(),
        P(),
        P(),
        P(),
        P(("tok", "exp"), None),
        P(),
        P(("tok", "exp"), None),
        P(("tok", "exp"), None),
        P("tok", None, "exp"),
        P("tok", None, "exp"),
        P("tok", "exp", None),
    )
    out_specs = P(("tok", "exp"), None)
    return jax.shard_map(shards, mesh=mesh, in_specs=in_specs, out_specs=out_specs, check_vma=False)
```

```python
import jax
import jax.numpy as jnp
from jax import lax
from jax.experimental import pallas as pl
from jax.experimental.pallas import tpu as pltpu
from jax.sharding import PartitionSpec as P

MESH = pl.DeviceIdType.MESH
BF16 = jnp.bfloat16
F32 = jnp.float32
D = 1024
H = 16
VARS = 3
ROWS = 128
EXPERTS = 64
GROUP = 4
FF = 256
CAP = 7
NT = 16
NZ = 4
BLK = NT * CAP
HALF = NZ * BLK
WIDE = D // 2
HH = H // 2
MSG = NT * 16
MSG_SENT = MSG - 16
XSLOTS = 3
FIRST_Z = 3


def dot(a, b):
    return jnp.dot(a, b, preferred_element_type=F32)


def dot_t(a, b):
    return lax.dot_general(a, b, (((0,), (0,)), ((), ())), preferred_element_type=F32)


def iota(shape, dim):
    return lax.broadcasted_iota(jnp.int32, shape, dim)


def kernel(
    x,
    ids,
    embed,
    svec,
    vw,
    ow,
    half,
    gain,
    routes,
    rweights,
    wg,
    wu,
    wd,
    out,
    wgu,
    wdn,
    vwb,
    owb,
    xbuf,
    hbuf,
    lab,
    svp,
    spread,
    comb,
    pk,
    rb,
    zq,
    rbq,
    ag,
    pt,
    sb,
    zr1,
    zr2,
    so,
    rs,
    rr,
    ns,
    n1r,
    n2s,
    n2r,
    st_s,
    st1r,
    st2s,
    st2r,
    acc,
    xsem,
    wsem,
    a_s,
    a_r,
    q_s,
    q_r,
    qx_s,
    qx_r,
    g_s,
    g_r,
    p_s,
    p_r,
    r_s,
    r_r,
    n1_s,
    n1_r,
    t1_s,
    t1_r,
    n2_s,
    n2_r,
    t2_s,
    t2_r,
):
    me = lax.axis_index("tok")
    ex = lax.axis_index("exp")
    z = ex // 2
    core = ex % 2
    y = me // 4
    xx = me % 4
    up = (me, ((z + 1) % NZ) * 2 + core)
    down = (me, ((z + NZ - 1) % NZ) * 2 + core)
    sib = (me, z * 2 + (1 - core))

    def tok_dev(o):
        return ((me + o) % NT, ex)

    def remote(src, dst, send, recv, dev):
        return pltpu.make_async_remote_copy(
            src_ref=src, dst_ref=dst, send_sem=send, recv_sem=recv, device_id=dev, device_id_type=MESH
        )

    def rows_at(start, size):
        return pl.ds(pl.multiple_of(start, 16), size)

    def along_x(dx):
        return (y * 4 + (xx + dx) % 4, ex)

    def along_y(dy):
        return (((y + dy) % 4) * 4 + xx, ex)

    def offsets(o):
        return (o + 1 + o // 4) % 4, (o + 1) % 4

    def x_copy(o):
        slot = o % XSLOTS
        dy, dx = offsets(o)
        dest = ((y + dy) % 4) * 4 + (xx + dx) % 4
        return pltpu.make_async_copy(x.at[:, dest], xbuf.at[slot], xsem.at[slot])

    vw_copy = pltpu.make_async_copy(vw, vwb, wsem.at[0])
    ow_copy = pltpu.make_async_copy(ow, owb, wsem.at[1])
    w_copies = []
    for e in range(GROUP):
        w_copies.append(
            (
                pltpu.make_async_copy(wg.at[e], wgu.at[e, :, 0:FF], wsem.at[2 + 3 * e]),
                pltpu.make_async_copy(wu.at[e], wgu.at[e, :, FF : 2 * FF], wsem.at[3 + 3 * e]),
                pltpu.make_async_copy(wd.at[e], wdn.at[e], wsem.at[4 + 3 * e]),
            )
        )

    half_copy = pltpu.make_async_copy(half, hbuf, wsem.at[2 + 3 * GROUP])
    half_copy.start()
    barrier = pltpu.get_barrier_semaphore()
    greeted = [tok_dev(o) for o in range(1, NT)] + [up, down, sib]
    for dev in greeted:
        pl.semaphore_signal(barrier, inc=1, device_id=dev, device_id_type=MESH)

    vw_copy.start()
    for o in range(XSLOTS):
        x_copy(o).start()
    for group in w_copies:
        for copy in group:
            copy.start()
    ow_copy.start()

    route0 = routes[0:1, :]
    route1 = routes[1:2, :]
    experts = iota((EXPERTS, ROWS), 0)
    named0 = route0 == experts
    named1 = route1 == experts
    either = jnp.where(named0 | named1, 1.0, 0.0).astype(BF16)
    before = jnp.where(iota((ROWS, ROWS), 0) < iota((ROWS, ROWS), 1), 1.0, 0.0).astype(BF16)
    count = dot(either, before)

    def target(route, named):
        slot = jnp.sum(jnp.where(named, count, 0.0), axis=0, keepdims=True).astype(jnp.int32)
        return route * 8 + slot

    target0 = target(route0, named0)
    target1 = target(route1, named1)
    half_copy.wait()
    level = hbuf[...].astype(F32)
    scale = lax.rsqrt(jnp.mean(level * level, axis=-1, keepdims=True) + 1e-06)
    normed = (level * scale * gain[...].astype(F32).reshape(1, D)).astype(BF16)
    msg_row = iota((MSG, ROWS), 0)
    msg_key = jnp.right_shift(msg_row, 4) * (GROUP * 8) + (msg_row & 7)
    second = (jnp.right_shift(iota((MSG, WIDE), 0), 3) & 1) == 1

    def halves(full):
        return jnp.where(second, full[:, WIDE:], full[:, :WIDE]).astype(BF16)

    def here(e):
        return msg_key == target0 - e * 8, msg_key == target1 - e * 8

    def pack(e):
        here0, here1 = here(e)
        placing = jnp.where(here0 | here1, 1.0, 0.0).astype(BF16)
        pk[e] = halves(dot(placing, normed))

    pack(FIRST_Z)
    pack(0)
    pl.semaphore_wait(barrier, len(greeted))

    def landed(place, sem):
        pltpu.make_async_copy(place, place, sem).wait()

    def msg(i):
        return rows_at(i * 16, 16)

    def dispatch(e, o):
        there = (me + o) % NT
        return remote(pk.at[e, msg(there)], rb.at[e, msg(me)], a_s.at[e], a_r.at[e], tok_dev(o))

    def along_z(kind):
        half_rows = MSG // 2
        src, dst, dev = {
            0: (pk.at[FIRST_Z], zq.at[2], up),
            1: (pk.at[FIRST_Z], zq.at[0], down),
            2: (zq.at[2, 0:half_rows], zq.at[1, 0:half_rows], up),
            3: (zq.at[0, half_rows:MSG], zq.at[1, half_rows:MSG], down),
        }[kind]
        return remote(src, dst, q_s.at[0], q_r.at[min(kind, 2)], dev)

    def dispatch_z(o):
        there = (me + o) % NT
        return remote(zq.at[:, msg(there)], rbq.at[:, msg(me)], qx_s.at[0], qx_r.at[0], tok_dev(o))

    along_z(0).start()
    along_z(1).start()
    for e in range(GROUP):
        if 0 < e < FIRST_Z:
            pack(e)
        for o in range(1, NT):
            dispatch(e, o).start()

    def z_second():
        landed(zq.at[2], q_r.at[0])
        along_z(2).start()
        landed(zq.at[0], q_r.at[1])
        along_z(3).start()

    def z_third():
        landed(zq.at[1], q_r.at[2])
        for o in range(1, NT):
            dispatch_z(o).start()

    def dispatch_arrived(e):
        landed(rb.at[e, 0:MSG_SENT], a_r.at[e])
        rb[e, msg(me)] = pk[e, msg(me)]

    msg_half = jnp.right_shift(msg_row, 3) & 1
    for e in range(GROUP):
        here0, here1 = here(e)
        weights = jnp.where(here0, rweights[0:1, :], 0.0) + jnp.where(here1, rweights[1:2, :], 0.0)
        for side in range(2):
            turned = jnp.transpose(jnp.where(msg_half == side, weights, 0.0))
            high = turned.astype(BF16)
            comb[e, side, 0:ROWS] = high
            comb[e, side, ROWS : 2 * ROWS] = (turned - high.astype(F32)).astype(BF16)

    picks = jnp.where(ids[...] == iota((embed.shape[0], VARS), 0), 1.0, 0.0).astype(BF16)
    lab[0:VARS] = dot_t(picks, embed[...])
    turned_scores = jnp.concatenate([svec[...].astype(F32), jnp.zeros((128 - H, D), F32)], axis=0)
    svp[...] = jnp.transpose(turned_scores).astype(BF16)
    spread[...] = jnp.where(jnp.right_shift(iota((H, D), 1), 6) == iota((H, D), 0), 1.0, 0.0).astype(BF16)
    vw_copy.wait()

    def sum_one(side, dy, dx):
        k = dy * 4 + dx
        if side == 0:
            d, first, dev = dy, dx - 1, along_x(dx)
        else:
            d, first, dev = dx, dy - 1, along_y(dy)
        return (
            remote(ns.at[k, side], n1r.at[side, d, first], n1_s.at[side], n1_r.at[side, d], dev),
            remote(st_s.at[k, side], st1r.at[side, d, first], t1_s.at[side], t1_r.at[side, d], dev),
        )

    def sum_two(side, d):
        dev = along_y(d) if side == 0 else along_x(d)
        return (
            remote(n2s.at[side, d], n2r.at[side, d - 1], n2_s.at[side], n2_r.at[side], dev),
            remote(st2s.at[side, d], st2r.at[side, d - 1], t2_s.at[side], t2_r.at[side], dev),
        )

    def aggregate(o, _):
        dy, dx = offsets(o)
        k = dy * 4 + dx
        slot = o % XSLOTS
        x_copy(o).wait()
        embedded = jnp.concatenate(
            [(xbuf[slot, v].astype(F32) + lab[v : v + 1]).astype(BF16) for v in range(VARS)], axis=0
        )
        scores = dot(embedded, svp[...])
        parts = [jnp.transpose(scores[v * ROWS : (v + 1) * ROWS])[0:H] for v in range(VARS)]
        peak = jnp.maximum(jnp.maximum(parts[0], parts[1]), parts[2])
        expo = [jnp.exp(part - peak) for part in parts]
        denom = expo[0] + expo[1] + expo[2]
        inverse = 1.0 / denom
        for side in range(2):
            st_s[k, side, 0:HH] = peak[side * HH : (side + 1) * HH]
            st_s[k, side, HH : 2 * HH] = denom[side * HH : (side + 1) * HH]
        values = dot(embedded, vwb[...])
        mixed = None
        for v in range(VARS):
            share = dot_t((expo[v] * inverse).astype(BF16), spread[...])
            term = share * values[v * ROWS : (v + 1) * ROWS]
            mixed = term if mixed is None else mixed + term
        ns[k, 0] = mixed[:, :WIDE].astype(BF16)
        ns[k, 1] = mixed[:, WIDE:].astype(BF16)

        @pl.when(dx > 0)
        def _():
            for copy in sum_one(0, dy, dx):
                copy.start()

        @pl.when(dy > 0)
        def _():
            for copy in sum_one(1, dy, dx):
                copy.start()

        @pl.when(o + XSLOTS < NT)
        def _():
            x_copy(o + XSLOTS).start()

        return 0

    def aggregate_range(low, high_):
        lax.fori_loop(low, high_, aggregate, 0)

    mine_ag = (core * NZ + z) * BLK

    def packed_row(row):
        return jnp.where((row & 7) < CAP, jnp.right_shift(row, 4) * CAP + (row & 7), -1)

    def compact(e, row=mine_ag, source=None):
        col = iota((BLK, MSG), 1)
        match = iota((BLK, MSG), 0) == packed_row(col)
        rows = rb[e] if source is None else source
        for side in range(2):
            pick = jnp.where(match & ((jnp.right_shift(col, 3) & 1) == side), 1.0, 0.0).astype(BF16)
            ag[e, rows_at(row, BLK), side * WIDE : (side + 1) * WIDE] = dot(pick, rows).astype(BF16)

    def low_rows(e):
        return 64 if e % 2 == 0 else 48

    def block_row(c, dz):
        return (c * NZ + (z + dz) % NZ) * BLK

    def gather_copy(e, kind):
        low = low_rows(e)
        start, size, dev = {
            0: (block_row(core, 0), BLK, up),
            1: (block_row(core, 0), BLK, down),
            2: (block_row(core, NZ - 1), low, up),
            3: (block_row(core, 1) + low, BLK - low, down),
            4: (block_row(core, 0), BLK, sib),
            5: (block_row(core, NZ - 1), BLK, sib),
            6: (block_row(core, 1), BLK, sib),
            7: (block_row(core, 2), low, sib),
            8: (block_row(core, 2) + low, BLK - low, sib),
        }[kind]
        place = ag.at[e, rows_at(start, size)]
        return remote(place, place, g_s.at[e], g_r.at[e, min(kind, 4)], dev)

    def gather_recv(e, kind):
        low = low_rows(e)
        start, size = {
            0: (block_row(core, NZ - 1), BLK),
            1: (block_row(core, 1), BLK),
            2: (block_row(core, 2), low),
            3: (block_row(core, 2) + low, BLK - low),
            4: ((1 - core) * HALF, HALF),
        }[kind]
        landed(ag.at[e, rows_at(start, size)], g_r.at[e, kind])

    def gather_first(e):
        gather_copy(e, 0).start()
        gather_copy(e, 1).start()
        gather_copy(e, 4).start()

    def gather_second(e):
        gather_recv(e, 0)
        gather_copy(e, 2).start()
        gather_copy(e, 5).start()
        gather_recv(e, 1)
        gather_copy(e, 3).start()
        gather_copy(e, 6).start()

    def gather_third(e):
        gather_recv(e, 2)
        gather_copy(e, 7).start()
        gather_recv(e, 3)
        gather_copy(e, 8).start()

    def all_copy():
        place = ag.at[FIRST_Z, rows_at(core * HALF, HALF)]
        return remote(place, place, g_s.at[FIRST_Z], g_r.at[FIRST_Z, 4], sib)

    def z_arrived():
        dispatch_arrived(FIRST_Z)
        compact(FIRST_Z)
        landed(rbq.at[:, 0:MSG_SENT], qx_r.at[0])
        rbq[:, msg(me)] = zq[:, msg(me)]
        for dz in range(1, NZ):
            compact(FIRST_Z, block_row(core, dz), rbq[dz - 1])
        all_copy().start()

    def ffn(e, start):
        rows = rows_at(start, HALF)
        both = dot(ag[e, rows], wgu[e])
        gate = both[:, 0:FF]
        hidden = (gate / (1.0 + jnp.exp(-gate)) * both[:, FF : 2 * FF]).astype(BF16)
        pt[e, rows] = dot(hidden, wdn[e]).astype(BF16)

    def sibling_copy(e):
        return remote(
            pt.at[e, rows_at((1 - core) * HALF, HALF)], sb.at[e], p_s.at[e], p_r.at[e, 0], sib
        )

    def experts_of(e):
        for copy in w_copies[e]:
            copy.wait()
        ffn(e, core * HALF)
        gather_recv(e, 4)
        ffn(e, (1 - core) * HALF)
        sibling_copy(e).start()

    def part(e, dz, start, size):
        return pt.at[e, rows_at(block_row(core, dz) + start, size)]

    def sum_step(e, kind):
        low = low_rows(e)
        src, dst, dev = {
            1: (part(e, 2, 0, low), zr1.at[e, 0, 0:low], up),
            2: (part(e, 2, low, BLK - low), zr1.at[e, 1, 0 : BLK - low], down),
            3: (part(e, 1, low, BLK - low), zr2.at[e, 0, low:BLK], up),
            4: (part(e, 1, 0, low), zr2.at[e, 0, 0:low], up),
            5: (part(e, NZ - 1, 0, low), zr2.at[e, 1, 0:low], down),
            6: (part(e, NZ - 1, low, BLK - low), zr2.at[e, 1, low:BLK], down),
        }[kind]
        return remote(src, dst, p_s.at[e], p_r.at[e, min(kind, 3)], dev)

    def add_sibling(e, dz):
        here = rows_at(block_row(core, dz), BLK)
        there = rows_at(((z + dz) % NZ) * BLK, BLK)
        pt[e, here] = (pt[e, here].astype(F32) + sb[e, there].astype(F32)).astype(BF16)

    def sum_first(e):
        landed(sb.at[e], p_r.at[e, 0])
        add_sibling(e, 2)
        sum_step(e, 1).start()
        sum_step(e, 2).start()
        add_sibling(e, 1)
        sum_step(e, 3).start()
        add_sibling(e, NZ - 1)
        sum_step(e, 5).start()
        add_sibling(e, 0)

    def sum_second(e):
        low = low_rows(e)
        landed(zr1.at[e, 0, 0:low], p_r.at[e, 1])
        here = rows_at(block_row(core, 1), low)
        pt[e, here] = (pt[e, here].astype(F32) + zr1[e, 0, 0:low].astype(F32)).astype(BF16)
        sum_step(e, 4).start()
        landed(zr1.at[e, 1, 0 : BLK - low], p_r.at[e, 2])
        here = rows_at(block_row(core, NZ - 1) + low, BLK - low)
        pt[e, here] = (pt[e, here].astype(F32) + zr1[e, 1, 0 : BLK - low].astype(F32)).astype(BF16)
        sum_step(e, 6).start()

    def sum_third(e):
        landed(zr2.at[e], p_r.at[e, 3])
        here = rows_at(block_row(core, 0), BLK)
        total = pt[e, here].astype(F32) + zr2[e, 0].astype(F32) + zr2[e, 1].astype(F32)
        so[...] = total.astype(BF16)
        send_back(e)

    def give_back(e, o):
        there = (me + o) % NT
        return remote(rs.at[e, msg(there)], rr.at[e, msg(me)], r_s.at[e], r_r.at[e], tok_dev(o))

    def send_back(e):
        place = jnp.where(
            iota((MSG, BLK), 1) == packed_row(iota((MSG, BLK), 0)), 1.0, 0.0
        ).astype(BF16)
        rs[e] = halves(dot(place, so[...]))
        for o in range(1, NT):
            give_back(e, o).start()

    def merged(stats, sums):
        peak = stats[0][0:HH]
        for stat in stats[1:]:
            peak = jnp.maximum(peak, stat[0:HH])
        shares = [stat[HH : 2 * HH] * jnp.exp(stat[0:HH] - peak) for stat in stats]
        total = shares[0] + shares[1] + shares[2] + shares[3]
        inverse = 1.0 / total
        value = None
        for share, term in zip(shares, sums):
            wide = dot_t((share * inverse).astype(BF16), spread[0:HH, 0:WIDE])
            piece = wide * term.astype(F32)
            value = piece if value is None else value + piece
        return peak, total, value

    def merge_one(side, d):
        stats, sums = [], []
        k = d * 4 if side == 0 else d
        stats.append(st_s[k, side])
        sums.append(ns[k, side])
        landed(st1r.at[side, d], t1_r.at[side, d])
        landed(n1r.at[side, d], n1_r.at[side, d])
        for first in range(3):
            stats.append(st1r[side, d, first])
            sums.append(n1r[side, d, first])
        peak, total, value = merged(stats, sums)
        st2s[side, d, 0:HH] = peak
        st2s[side, d, HH : 2 * HH] = total
        n2s[side, d] = value.astype(BF16)
        if d > 0:
            for copy in sum_two(side, d):
                copy.start()

    def merge_two():
        for side in range(2):
            stats, sums = [st2s[side, 0]], [n2s[side, 0]]
            landed(st2r.at[side], t2_r.at[side])
            landed(n2r.at[side], n2_r.at[side])
            for d in range(1, 4):
                stats.append(st2r[side, d - 1])
                sums.append(n2r[side, d - 1])
            acc[:, side * WIDE : (side + 1) * WIDE] = merged(stats, sums)[2]
        ow_copy.wait()
        acc[...] = dot(acc[...].astype(BF16), owb[...])

    def take_back(e):
        landed(rr.at[e, 0:MSG_SENT], r_r.at[e])
        rr[e, msg(me)] = rs[e, msg(me)]
        for side in range(2):
            both = dot(comb[e, side], rr[e])
            acc[:, side * WIDE : (side + 1) * WIDE] += both[0:ROWS] + both[ROWS : 2 * ROWS]

    aggregate_range(0, 3)
    z_second()
    dispatch_arrived(0)
    compact(0)
    gather_first(0)
    dispatch_arrived(1)
    compact(1)
    gather_first(1)
    aggregate_range(3, 7)
    z_third()
    dispatch_arrived(2)
    compact(2)
    gather_second(0)
    gather_first(2)
    aggregate_range(7, 11)
    gather_second(1)
    gather_third(0)
    aggregate_range(11, 12)
    experts_of(0)
    aggregate_range(12, 14)
    gather_second(2)
    sum_first(0)
    gather_third(1)
    experts_of(1)
    aggregate_range(14, 16)
    sum_second(0)
    sum_first(1)
    gather_third(2)
    experts_of(2)
    for d in range(1, 4):
        merge_one(0, d)
        merge_one(1, d)
    sum_third(0)
    sum_second(1)
    sum_first(2)
    z_arrived()
    experts_of(3)
    merge_one(0, 0)
    merge_one(1, 0)
    sum_third(1)
    sum_second(2)
    sum_first(3)
    sum_third(2)
    sum_second(3)
    merge_two()
    take_back(0)
    take_back(1)
    sum_third(3)
    take_back(2)
    take_back(3)
    out[...] = acc[...].astype(BF16)

    landed(zq.at[:], q_s.at[0])
    landed(rbq.at[:, 0:MSG_SENT], qx_s.at[0])
    for e in range(GROUP):
        landed(pk.at[e, 0:MSG_SENT], a_s.at[e])
        landed(rs.at[e, 0:MSG_SENT], r_s.at[e])
        sent = 4 if e == FIRST_Z else 7
        landed(ag.at[e, 0 : sent * BLK], g_s.at[e])
        landed(pt.at[e, 0 : 7 * BLK], p_s.at[e])
    for side in range(2):
        landed(n1r.at[side], n1_s.at[side])
        landed(st1r.at[side], t1_s.at[side])
        landed(n2r.at[side], n2_s.at[side])
        landed(st2r.at[side], t2_s.at[side])


def shards(
    x_var,
    var_ids,
    var_embed,
    score_vecs,
    v_weight,
    out_weight,
    second_half,
    norm_gain,
    routes,
    route_weights,
    w_gate,
    w_up,
    w_down,
):
    vmem = pl.BlockSpec(memory_space=pltpu.VMEM)
    anywhere = pl.BlockSpec(memory_space=pl.ANY)
    dma = pltpu.SemaphoreType.DMA
    return pl.pallas_call(
        kernel,
        out_shape=jax.ShapeDtypeStruct((ROWS, D), BF16),
        in_specs=[
            anywhere,
            vmem,
            vmem,
            vmem,
            anywhere,
            anywhere,
            anywhere,
            vmem,
            vmem,
            vmem,
            anywhere,
            anywhere,
            anywhere,
        ],
        out_specs=vmem,
        scratch_shapes=[
            pltpu.VMEM((GROUP, D, 2 * FF), BF16),
            pltpu.VMEM((GROUP, FF, D), BF16),
            pltpu.VMEM((D, D), BF16),
            pltpu.VMEM((D, D), BF16),
            pltpu.VMEM((XSLOTS, VARS, ROWS, D), BF16),
            pltpu.VMEM((ROWS, D), BF16),
            pltpu.VMEM((8, D), F32),
            pltpu.VMEM((D, 128), BF16),
            pltpu.VMEM((H, D), BF16),
            pltpu.VMEM((GROUP, 2, 2 * ROWS, MSG), BF16),
            pltpu.VMEM((GROUP, MSG, WIDE), BF16),
            pltpu.VMEM((GROUP, MSG, WIDE), BF16),
            pltpu.VMEM((NZ - 1, MSG, WIDE), BF16),
            pltpu.VMEM((NZ - 1, MSG, WIDE), BF16),
            pltpu.VMEM((GROUP, 2 * HALF, D), BF16),
            pltpu.VMEM((GROUP, 2 * HALF, D), BF16),
            pltpu.VMEM((GROUP, HALF, D), BF16),
            pltpu.VMEM((GROUP, 2, 64, D), BF16),
            pltpu.VMEM((GROUP, 2, BLK, D), BF16),
            pltpu.VMEM((BLK, D), BF16),
            pltpu.VMEM((GROUP, MSG, WIDE), BF16),
            pltpu.VMEM((GROUP, MSG, WIDE), BF16),
            pltpu.VMEM((NT, 2, ROWS, WIDE), BF16),
            pltpu.VMEM((2, 4, 3, ROWS, WIDE), BF16),
            pltpu.VMEM((2, 4, ROWS, WIDE), BF16),
            pltpu.VMEM((2, 3, ROWS, WIDE), BF16),
            pltpu.VMEM((NT, 2, H, ROWS), F32),
            pltpu.VMEM((2, 4, 3, H, ROWS), F32),
            pltpu.VMEM((2, 4, H, ROWS), F32),
            pltpu.VMEM((2, 3, H, ROWS), F32),
            pltpu.VMEM((ROWS, D), F32),
            dma((XSLOTS,)),
            dma((3 + 3 * GROUP,)),
            dma((GROUP,)),
            dma((GROUP,)),
            dma((1,)),
            dma((3,)),
            dma((1,)),
            dma((1,)),
            dma((GROUP,)),
            dma((GROUP, 5)),
            dma((GROUP,)),
            dma((GROUP, 4)),
            dma((GROUP,)),
            dma((GROUP,)),
            dma((2,)),
            dma((2, 4)),
            dma((2,)),
            dma((2, 4)),
            dma((2,)),
            dma((2,)),
            dma((2,)),
            dma((2,)),
        ],
        compiler_params=pltpu.CompilerParams(
            collective_id=0, has_side_effects=True, vmem_limit_bytes=62 * 2**20
        ),
        cost_estimate=pl.CostEstimate(
            flops=20_000_000_000, bytes_accessed=24_000_000, transcendentals=1_000_000
        ),
    )(
        x_var,
        var_ids.reshape(1, VARS),
        var_embed,
        score_vecs.T,
        v_weight,
        out_weight,
        second_half,
        norm_gain,
        routes.T,
        route_weights.T,
        w_gate,
        w_up,
        w_down,
    )


def solution(mesh):
    in_specs = (
        P("tok", None, "exp", None),
        P("tok"),
        P(),
        P(),
        P(),
        P(),
        P(("tok", "exp"), None),
        P(),
        P(("tok", "exp"), None),
        P(("tok", "exp"), None),
        P("tok", None, "exp"),
        P("tok", None, "exp"),
        P("tok", "exp", None),
    )
    out_specs = P(("tok", "exp"), None)
    return jax.shard_map(shards, mesh=mesh, in_specs=in_specs, out_specs=out_specs, check_vma=False)
```

```python
import jax
import jax.numpy as jnp
from jax import lax
from jax.experimental import pallas as pl
from jax.experimental.pallas import tpu as pltpu
from jax.sharding import PartitionSpec as P

MESH = pl.DeviceIdType.MESH
BF16 = jnp.bfloat16
F32 = jnp.float32
D = 1024
H = 16
VARS = 3
ROWS = 128
EXPERTS = 64
GROUP = 4
FF = 256
CAP = 7
NT = 16
NZ = 4
BLK = NT * CAP
HALF = NZ * BLK
WIDE = D // 2
HH = H // 2
MSG = NT * 16
MSG_SENT = MSG - 16
XSLOTS = 3
FIRST_Z = 3


def dot(a, b):
    return jnp.dot(a, b, preferred_element_type=F32)


def dot_t(a, b):
    return lax.dot_general(a, b, (((0,), (0,)), ((), ())), preferred_element_type=F32)


def iota(shape, dim):
    return lax.broadcasted_iota(jnp.int32, shape, dim)


def kernel(
    x,
    ids,
    embed,
    svec,
    vw,
    ow,
    half,
    gain,
    routes,
    rweights,
    wg,
    wu,
    wd,
    out,
    wgu,
    wdn,
    vwb,
    owb,
    xbuf,
    hbuf,
    lab,
    svp,
    spread,
    comb,
    pk,
    rb,
    zq,
    rbq,
    ag,
    pt,
    sb,
    zr1,
    zr2,
    so,
    rs,
    rr,
    ns,
    n1r,
    n2s,
    n2r,
    st_s,
    st1r,
    st2s,
    st2r,
    acc,
    xsem,
    wsem,
    a_s,
    a_r,
    q_s,
    q_r,
    qx_s,
    qx_r,
    g_s,
    g_r,
    p_s,
    p_r,
    r_s,
    r_r,
    n1_s,
    n1_r,
    t1_s,
    t1_r,
    n2_s,
    n2_r,
    t2_s,
    t2_r,
):
    me = lax.axis_index("tok")
    ex = lax.axis_index("exp")
    z = ex // 2
    core = ex % 2
    y = me // 4
    xx = me % 4
    up = (me, ((z + 1) % NZ) * 2 + core)
    down = (me, ((z + NZ - 1) % NZ) * 2 + core)
    sib = (me, z * 2 + (1 - core))

    def tok_dev(o):
        return ((me + o) % NT, ex)

    def remote(src, dst, send, recv, dev):
        return pltpu.make_async_remote_copy(
            src_ref=src, dst_ref=dst, send_sem=send, recv_sem=recv, device_id=dev, device_id_type=MESH
        )

    def rows_at(start, size):
        return pl.ds(pl.multiple_of(start, 16), size)

    def along_x(dx):
        return (y * 4 + (xx + dx) % 4, ex)

    def along_y(dy):
        return (((y + dy) % 4) * 4 + xx, ex)

    def offsets(o):
        return (o + 1 + o // 4) % 4, (o + 1) % 4

    def x_copy(o):
        slot = o % XSLOTS
        dy, dx = offsets(o)
        dest = ((y + dy) % 4) * 4 + (xx + dx) % 4
        return pltpu.make_async_copy(x.at[:, dest], xbuf.at[slot], xsem.at[slot])

    vw_copy = pltpu.make_async_copy(vw, vwb, wsem.at[0])
    ow_copy = pltpu.make_async_copy(ow, owb, wsem.at[1])
    w_copies = []
    for e in range(GROUP):
        w_copies.append(
            (
                pltpu.make_async_copy(wg.at[e], wgu.at[e, :, 0:FF], wsem.at[2 + 3 * e]),
                pltpu.make_async_copy(wu.at[e], wgu.at[e, :, FF : 2 * FF], wsem.at[3 + 3 * e]),
                pltpu.make_async_copy(wd.at[e], wdn.at[e], wsem.at[4 + 3 * e]),
            )
        )

    half_copy = pltpu.make_async_copy(half, hbuf, wsem.at[2 + 3 * GROUP])
    half_copy.start()
    barrier = pltpu.get_barrier_semaphore()
    greeted = [tok_dev(o) for o in range(1, NT)] + [up, down, sib]
    for dev in greeted:
        pl.semaphore_signal(barrier, inc=1, device_id=dev, device_id_type=MESH)

    vw_copy.start()
    for o in range(XSLOTS):
        x_copy(o).start()
    for group in w_copies:
        for copy in group:
            copy.start()
    ow_copy.start()

    route0 = routes[0:1, :]
    route1 = routes[1:2, :]
    experts = iota((EXPERTS, ROWS), 0)
    named0 = route0 == experts
    named1 = route1 == experts
    either = jnp.where(named0 | named1, 1.0, 0.0).astype(BF16)
    before = jnp.where(iota((ROWS, ROWS), 0) < iota((ROWS, ROWS), 1), 1.0, 0.0).astype(BF16)
    count = dot(either, before)

    def target(route, named):
        slot = jnp.sum(jnp.where(named, count, 0.0), axis=0, keepdims=True).astype(jnp.int32)
        return route * 8 + slot

    target0 = target(route0, named0)
    target1 = target(route1, named1)
    half_copy.wait()
    level = hbuf[...].astype(F32)
    scale = lax.rsqrt(jnp.mean(level * level, axis=-1, keepdims=True) + 1e-06)
    normed = (level * scale * gain[...].astype(F32).reshape(1, D)).astype(BF16)
    msg_row = iota((MSG, ROWS), 0)
    msg_key = jnp.right_shift(msg_row, 4) * (GROUP * 8) + (msg_row & 7)
    second = (jnp.right_shift(iota((MSG, WIDE), 0), 3) & 1) == 1

    def halves(full):
        return jnp.where(second, full[:, WIDE:], full[:, :WIDE]).astype(BF16)

    def here(e):
        return msg_key == target0 - e * 8, msg_key == target1 - e * 8

    def pack(e):
        here0, here1 = here(e)
        placing = jnp.where(here0 | here1, 1.0, 0.0).astype(BF16)
        pk[e] = halves(dot(placing, normed))

    pack(FIRST_Z)
    pack(0)
    pl.semaphore_wait(barrier, len(greeted))

    def landed(place, sem):
        pltpu.make_async_copy(place, place, sem).wait()

    def msg(i):
        return rows_at(i * 16, 16)

    def dispatch(e, o):
        there = (me + o) % NT
        return remote(pk.at[e, msg(there)], rb.at[e, msg(me)], a_s.at[e], a_r.at[e], tok_dev(o))

    def along_z(kind):
        half_rows = MSG // 2
        src, dst, dev = {
            0: (pk.at[FIRST_Z], zq.at[2], up),
            1: (pk.at[FIRST_Z], zq.at[0], down),
            2: (zq.at[2, 0:half_rows], zq.at[1, 0:half_rows], up),
            3: (zq.at[0, half_rows:MSG], zq.at[1, half_rows:MSG], down),
        }[kind]
        return remote(src, dst, q_s.at[0], q_r.at[min(kind, 2)], dev)

    def dispatch_z(o):
        there = (me + o) % NT
        return remote(zq.at[:, msg(there)], rbq.at[:, msg(me)], qx_s.at[0], qx_r.at[0], tok_dev(o))

    along_z(0).start()
    along_z(1).start()
    for e in range(GROUP):
        if 0 < e < FIRST_Z:
            pack(e)
        for o in range(1, NT):
            dispatch(e, o).start()

    def z_second():
        landed(zq.at[2], q_r.at[0])
        along_z(2).start()
        landed(zq.at[0], q_r.at[1])
        along_z(3).start()

    def z_third():
        landed(zq.at[1], q_r.at[2])
        for o in range(1, NT):
            dispatch_z(o).start()

    def dispatch_arrived(e):
        landed(rb.at[e, 0:MSG_SENT], a_r.at[e])
        rb[e, msg(me)] = pk[e, msg(me)]

    msg_half = jnp.right_shift(msg_row, 3) & 1
    for e in range(GROUP):
        here0, here1 = here(e)
        weights = jnp.where(here0, rweights[0:1, :], 0.0) + jnp.where(here1, rweights[1:2, :], 0.0)
        for side in range(2):
            turned = jnp.transpose(jnp.where(msg_half == side, weights, 0.0))
            high = turned.astype(BF16)
            comb[e, side, 0:ROWS] = high
            comb[e, side, ROWS : 2 * ROWS] = (turned - high.astype(F32)).astype(BF16)

    picks = jnp.where(ids[...] == iota((embed.shape[0], VARS), 0), 1.0, 0.0).astype(BF16)
    lab[0:VARS] = dot_t(picks, embed[...])
    turned_scores = jnp.concatenate([svec[...].astype(F32), jnp.zeros((128 - H, D), F32)], axis=0)
    svp[...] = jnp.transpose(turned_scores).astype(BF16)
    spread[...] = jnp.where(jnp.right_shift(iota((H, D), 1), 6) == iota((H, D), 0), 1.0, 0.0).astype(BF16)
    vw_copy.wait()

    def sum_one(side, dy, dx):
        k = dy * 4 + dx
        if side == 0:
            d, first, dev = dy, dx - 1, along_x(dx)
        else:
            d, first, dev = dx, dy - 1, along_y(dy)
        return (
            remote(ns.at[k, side], n1r.at[side, d, first], n1_s.at[side], n1_r.at[side, d], dev),
            remote(st_s.at[k, side], st1r.at[side, d, first], t1_s.at[side], t1_r.at[side, d], dev),
        )

    def sum_two(side, d):
        dev = along_y(d) if side == 0 else along_x(d)
        return (
            remote(n2s.at[side, d], n2r.at[side, d - 1], n2_s.at[side], n2_r.at[side], dev),
            remote(st2s.at[side, d], st2r.at[side, d - 1], t2_s.at[side], t2_r.at[side], dev),
        )

    def aggregate(o, _):
        dy, dx = offsets(o)
        k = dy * 4 + dx
        slot = o % XSLOTS
        x_copy(o).wait()
        embedded = jnp.concatenate(
            [(xbuf[slot, v].astype(F32) + lab[v : v + 1]).astype(BF16) for v in range(VARS)], axis=0
        )
        scores = dot(embedded, svp[...])
        parts = [jnp.transpose(scores[v * ROWS : (v + 1) * ROWS])[0:H] for v in range(VARS)]
        peak = jnp.maximum(jnp.maximum(parts[0], parts[1]), parts[2])
        expo = [jnp.exp(part - peak) for part in parts]
        denom = expo[0] + expo[1] + expo[2]
        inverse = 1.0 / denom
        for side in range(2):
            st_s[k, side, 0:HH] = peak[side * HH : (side + 1) * HH]
            st_s[k, side, HH : 2 * HH] = denom[side * HH : (side + 1) * HH]
        values = dot(embedded, vwb[...])
        mixed = None
        for v in range(VARS):
            share = dot_t((expo[v] * inverse).astype(BF16), spread[...])
            term = share * values[v * ROWS : (v + 1) * ROWS]
            mixed = term if mixed is None else mixed + term
        ns[k, 0] = mixed[:, :WIDE].astype(BF16)
        ns[k, 1] = mixed[:, WIDE:].astype(BF16)

        @pl.when(dx > 0)
        def _():
            for copy in sum_one(0, dy, dx):
                copy.start()

        @pl.when(dy > 0)
        def _():
            for copy in sum_one(1, dy, dx):
                copy.start()

        @pl.when(o + XSLOTS < NT)
        def _():
            x_copy(o + XSLOTS).start()

        return 0

    def aggregate_range(low, high_):
        lax.fori_loop(low, high_, aggregate, 0)

    mine_ag = (core * NZ + z) * BLK

    def packed_row(row):
        return jnp.where((row & 7) < CAP, jnp.right_shift(row, 4) * CAP + (row & 7), -1)

    def compact(e, row=mine_ag, source=None):
        col = iota((BLK, MSG), 1)
        match = iota((BLK, MSG), 0) == packed_row(col)
        rows = rb[e] if source is None else source
        for side in range(2):
            pick = jnp.where(match & ((jnp.right_shift(col, 3) & 1) == side), 1.0, 0.0).astype(BF16)
            ag[e, rows_at(row, BLK), side * WIDE : (side + 1) * WIDE] = dot(pick, rows).astype(BF16)

    def low_rows(e):
        return 64 if e % 2 == 0 else 48

    def block_row(c, dz):
        return (c * NZ + (z + dz) % NZ) * BLK

    def gather_copy(e, kind):
        low = low_rows(e)
        start, size, dev = {
            0: (block_row(core, 0), BLK, up),
            1: (block_row(core, 0), BLK, down),
            2: (block_row(core, NZ - 1), low, up),
            3: (block_row(core, 1) + low, BLK - low, down),
            4: (block_row(core, 0), BLK, sib),
            5: (block_row(core, NZ - 1), BLK, sib),
            6: (block_row(core, 1), BLK, sib),
            7: (block_row(core, 2), low, sib),
            8: (block_row(core, 2) + low, BLK - low, sib),
        }[kind]
        place = ag.at[e, rows_at(start, size)]
        return remote(place, place, g_s.at[e], g_r.at[e, min(kind, 4)], dev)

    def gather_recv(e, kind):
        low = low_rows(e)
        start, size = {
            0: (block_row(core, NZ - 1), BLK),
            1: (block_row(core, 1), BLK),
            2: (block_row(core, 2), low),
            3: (block_row(core, 2) + low, BLK - low),
            4: ((1 - core) * HALF, HALF),
        }[kind]
        landed(ag.at[e, rows_at(start, size)], g_r.at[e, kind])

    def gather_first(e):
        gather_copy(e, 0).start()
        gather_copy(e, 1).start()
        gather_copy(e, 4).start()

    def gather_second(e):
        gather_recv(e, 0)
        gather_copy(e, 2).start()
        gather_copy(e, 5).start()
        gather_recv(e, 1)
        gather_copy(e, 3).start()
        gather_copy(e, 6).start()

    def gather_third(e):
        gather_recv(e, 2)
        gather_copy(e, 7).start()
        gather_recv(e, 3)
        gather_copy(e, 8).start()

    def all_copy():
        place = ag.at[FIRST_Z, rows_at(core * HALF, HALF)]
        return remote(place, place, g_s.at[FIRST_Z], g_r.at[FIRST_Z, 4], sib)

    def z_arrived():
        dispatch_arrived(FIRST_Z)
        compact(FIRST_Z)
        landed(rbq.at[:, 0:MSG_SENT], qx_r.at[0])
        rbq[:, msg(me)] = zq[:, msg(me)]
        for dz in range(1, NZ):
            compact(FIRST_Z, block_row(core, dz), rbq[dz - 1])
        all_copy().start()

    def ffn(e, start):
        rows = rows_at(start, HALF)
        both = dot(ag[e, rows], wgu[e])
        gate = both[:, 0:FF]
        hidden = (gate / (1.0 + jnp.exp(-gate)) * both[:, FF : 2 * FF]).astype(BF16)
        pt[e, rows] = dot(hidden, wdn[e]).astype(BF16)

    def sibling_sem(e, dz):
        return p_r.at[e, {2: 0, 1: 4, 3: 5, 0: 6}[dz]]

    def sibling_copy(e, dz):
        src = pt.at[e, rows_at(block_row(1 - core, dz), BLK)]
        dst = sb.at[e, rows_at(((z + dz) % NZ) * BLK, BLK)]
        return remote(src, dst, p_s.at[e], sibling_sem(e, dz), sib)

    def experts_of(e):
        for copy in w_copies[e]:
            copy.wait()
        ffn(e, core * HALF)
        gather_recv(e, 4)
        ffn(e, (1 - core) * HALF)
        for dz in (2, 1, 3, 0):
            sibling_copy(e, dz).start()

    def part(e, dz, start, size):
        return pt.at[e, rows_at(block_row(core, dz) + start, size)]

    def sum_step(e, kind):
        low = low_rows(e)
        src, dst, dev = {
            1: (part(e, 2, 0, low), zr1.at[e, 0, 0:low], up),
            2: (part(e, 2, low, BLK - low), zr1.at[e, 1, 0 : BLK - low], down),
            3: (part(e, 1, low, BLK - low), zr2.at[e, 0, low:BLK], up),
            4: (part(e, 1, 0, low), zr2.at[e, 0, 0:low], up),
            5: (part(e, NZ - 1, 0, low), zr2.at[e, 1, 0:low], down),
            6: (part(e, NZ - 1, low, BLK - low), zr2.at[e, 1, low:BLK], down),
        }[kind]
        return remote(src, dst, p_s.at[e], p_r.at[e, min(kind, 3)], dev)

    def add_sibling(e, dz):
        here = rows_at(block_row(core, dz), BLK)
        there = rows_at(((z + dz) % NZ) * BLK, BLK)
        landed(sb.at[e, there], sibling_sem(e, dz))
        pt[e, here] = (pt[e, here].astype(F32) + sb[e, there].astype(F32)).astype(BF16)

    def sum_first(e):
        add_sibling(e, 2)
        sum_step(e, 1).start()
        sum_step(e, 2).start()
        add_sibling(e, 1)
        sum_step(e, 3).start()
        add_sibling(e, NZ - 1)
        sum_step(e, 5).start()
        add_sibling(e, 0)

    def sum_second(e):
        low = low_rows(e)
        landed(zr1.at[e, 0, 0:low], p_r.at[e, 1])
        here = rows_at(block_row(core, 1), low)
        pt[e, here] = (pt[e, here].astype(F32) + zr1[e, 0, 0:low].astype(F32)).astype(BF16)
        sum_step(e, 4).start()
        landed(zr1.at[e, 1, 0 : BLK - low], p_r.at[e, 2])
        here = rows_at(block_row(core, NZ - 1) + low, BLK - low)
        pt[e, here] = (pt[e, here].astype(F32) + zr1[e, 1, 0 : BLK - low].astype(F32)).astype(BF16)
        sum_step(e, 6).start()

    def sum_third(e):
        landed(zr2.at[e], p_r.at[e, 3])
        here = rows_at(block_row(core, 0), BLK)
        total = pt[e, here].astype(F32) + zr2[e, 0].astype(F32) + zr2[e, 1].astype(F32)
        so[...] = total.astype(BF16)
        send_back(e)

    def give_back(e, o):
        there = (me + o) % NT
        return remote(rs.at[e, msg(there)], rr.at[e, msg(me)], r_s.at[e], r_r.at[e], tok_dev(o))

    def send_back(e):
        place = jnp.where(
            iota((MSG, BLK), 1) == packed_row(iota((MSG, BLK), 0)), 1.0, 0.0
        ).astype(BF16)
        rs[e] = halves(dot(place, so[...]))
        for o in range(1, NT):
            give_back(e, o).start()

    def merged(stats, sums):
        peak = stats[0][0:HH]
        for stat in stats[1:]:
            peak = jnp.maximum(peak, stat[0:HH])
        shares = [stat[HH : 2 * HH] * jnp.exp(stat[0:HH] - peak) for stat in stats]
        total = shares[0] + shares[1] + shares[2] + shares[3]
        inverse = 1.0 / total
        value = None
        for share, term in zip(shares, sums):
            wide = dot_t((share * inverse).astype(BF16), spread[0:HH, 0:WIDE])
            piece = wide * term.astype(F32)
            value = piece if value is None else value + piece
        return peak, total, value

    def merge_one(side, d):
        stats, sums = [], []
        k = d * 4 if side == 0 else d
        stats.append(st_s[k, side])
        sums.append(ns[k, side])
        landed(st1r.at[side, d], t1_r.at[side, d])
        landed(n1r.at[side, d], n1_r.at[side, d])
        for first in range(3):
            stats.append(st1r[side, d, first])
            sums.append(n1r[side, d, first])
        peak, total, value = merged(stats, sums)
        st2s[side, d, 0:HH] = peak
        st2s[side, d, HH : 2 * HH] = total
        n2s[side, d] = value.astype(BF16)
        if d > 0:
            for copy in sum_two(side, d):
                copy.start()

    def merge_two():
        for side in range(2):
            stats, sums = [st2s[side, 0]], [n2s[side, 0]]
            landed(st2r.at[side], t2_r.at[side])
            landed(n2r.at[side], n2_r.at[side])
            for d in range(1, 4):
                stats.append(st2r[side, d - 1])
                sums.append(n2r[side, d - 1])
            acc[:, side * WIDE : (side + 1) * WIDE] = merged(stats, sums)[2]
        ow_copy.wait()
        acc[...] = dot(acc[...].astype(BF16), owb[...])

    def take_back(e):
        landed(rr.at[e, 0:MSG_SENT], r_r.at[e])
        rr[e, msg(me)] = rs[e, msg(me)]
        for side in range(2):
            both = dot(comb[e, side], rr[e])
            acc[:, side * WIDE : (side + 1) * WIDE] += both[0:ROWS] + both[ROWS : 2 * ROWS]

    aggregate_range(0, 3)
    z_second()
    dispatch_arrived(0)
    compact(0)
    gather_first(0)
    dispatch_arrived(1)
    compact(1)
    gather_first(1)
    aggregate_range(3, 7)
    z_third()
    dispatch_arrived(2)
    compact(2)
    gather_second(0)
    gather_first(2)
    aggregate_range(7, 11)
    gather_second(1)
    gather_third(0)
    aggregate_range(11, 12)
    experts_of(0)
    aggregate_range(12, 14)
    gather_second(2)
    sum_first(0)
    gather_third(1)
    experts_of(1)
    aggregate_range(14, 16)
    sum_second(0)
    sum_first(1)
    gather_third(2)
    experts_of(2)
    for d in range(1, 4):
        merge_one(0, d)
        merge_one(1, d)
    sum_third(0)
    sum_second(1)
    sum_first(2)
    z_arrived()
    experts_of(3)
    merge_one(0, 0)
    merge_one(1, 0)
    sum_third(1)
    sum_second(2)
    sum_first(3)
    sum_third(2)
    sum_second(3)
    merge_two()
    take_back(0)
    take_back(1)
    sum_third(3)
    take_back(2)
    take_back(3)
    out[...] = acc[...].astype(BF16)

    landed(zq.at[:], q_s.at[0])
    landed(rbq.at[:, 0:MSG_SENT], qx_s.at[0])
    for e in range(GROUP):
        landed(pk.at[e, 0:MSG_SENT], a_s.at[e])
        landed(rs.at[e, 0:MSG_SENT], r_s.at[e])
        sent = 4 if e == FIRST_Z else 7
        landed(ag.at[e, 0 : sent * BLK], g_s.at[e])
        landed(pt.at[e, 0 : 7 * BLK], p_s.at[e])
    for side in range(2):
        landed(n1r.at[side], n1_s.at[side])
        landed(st1r.at[side], t1_s.at[side])
        landed(n2r.at[side], n2_s.at[side])
        landed(st2r.at[side], t2_s.at[side])


def shards(
    x_var,
    var_ids,
    var_embed,
    score_vecs,
    v_weight,
    out_weight,
    second_half,
    norm_gain,
    routes,
    route_weights,
    w_gate,
    w_up,
    w_down,
):
    vmem = pl.BlockSpec(memory_space=pltpu.VMEM)
    anywhere = pl.BlockSpec(memory_space=pl.ANY)
    dma = pltpu.SemaphoreType.DMA
    return pl.pallas_call(
        kernel,
        out_shape=jax.ShapeDtypeStruct((ROWS, D), BF16),
        in_specs=[
            anywhere,
            vmem,
            vmem,
            vmem,
            anywhere,
            anywhere,
            anywhere,
            vmem,
            vmem,
            vmem,
            anywhere,
            anywhere,
            anywhere,
        ],
        out_specs=vmem,
        scratch_shapes=[
            pltpu.VMEM((GROUP, D, 2 * FF), BF16),
            pltpu.VMEM((GROUP, FF, D), BF16),
            pltpu.VMEM((D, D), BF16),
            pltpu.VMEM((D, D), BF16),
            pltpu.VMEM((XSLOTS, VARS, ROWS, D), BF16),
            pltpu.VMEM((ROWS, D), BF16),
            pltpu.VMEM((8, D), F32),
            pltpu.VMEM((D, 128), BF16),
            pltpu.VMEM((H, D), BF16),
            pltpu.VMEM((GROUP, 2, 2 * ROWS, MSG), BF16),
            pltpu.VMEM((GROUP, MSG, WIDE), BF16),
            pltpu.VMEM((GROUP, MSG, WIDE), BF16),
            pltpu.VMEM((NZ - 1, MSG, WIDE), BF16),
            pltpu.VMEM((NZ - 1, MSG, WIDE), BF16),
            pltpu.VMEM((GROUP, 2 * HALF, D), BF16),
            pltpu.VMEM((GROUP, 2 * HALF, D), BF16),
            pltpu.VMEM((GROUP, HALF, D), BF16),
            pltpu.VMEM((GROUP, 2, 64, D), BF16),
            pltpu.VMEM((GROUP, 2, BLK, D), BF16),
            pltpu.VMEM((BLK, D), BF16),
            pltpu.VMEM((GROUP, MSG, WIDE), BF16),
            pltpu.VMEM((GROUP, MSG, WIDE), BF16),
            pltpu.VMEM((NT, 2, ROWS, WIDE), BF16),
            pltpu.VMEM((2, 4, 3, ROWS, WIDE), BF16),
            pltpu.VMEM((2, 4, ROWS, WIDE), BF16),
            pltpu.VMEM((2, 3, ROWS, WIDE), BF16),
            pltpu.VMEM((NT, 2, H, ROWS), F32),
            pltpu.VMEM((2, 4, 3, H, ROWS), F32),
            pltpu.VMEM((2, 4, H, ROWS), F32),
            pltpu.VMEM((2, 3, H, ROWS), F32),
            pltpu.VMEM((ROWS, D), F32),
            dma((XSLOTS,)),
            dma((3 + 3 * GROUP,)),
            dma((GROUP,)),
            dma((GROUP,)),
            dma((1,)),
            dma((3,)),
            dma((1,)),
            dma((1,)),
            dma((GROUP,)),
            dma((GROUP, 5)),
            dma((GROUP,)),
            dma((GROUP, 7)),
            dma((GROUP,)),
            dma((GROUP,)),
            dma((2,)),
            dma((2, 4)),
            dma((2,)),
            dma((2, 4)),
            dma((2,)),
            dma((2,)),
            dma((2,)),
            dma((2,)),
        ],
        compiler_params=pltpu.CompilerParams(
            collective_id=0, has_side_effects=True, vmem_limit_bytes=62 * 2**20
        ),
        cost_estimate=pl.CostEstimate(
            flops=20_000_000_000, bytes_accessed=24_000_000, transcendentals=1_000_000
        ),
    )(
        x_var,
        var_ids.reshape(1, VARS),
        var_embed,
        score_vecs.T,
        v_weight,
        out_weight,
        second_half,
        norm_gain,
        routes.T,
        route_weights.T,
        w_gate,
        w_up,
        w_down,
    )


def solution(mesh):
    in_specs = (
        P("tok", None, "exp", None),
        P("tok"),
        P(),
        P(),
        P(),
        P(),
        P(("tok", "exp"), None),
        P(),
        P(("tok", "exp"), None),
        P(("tok", "exp"), None),
        P("tok", None, "exp"),
        P("tok", None, "exp"),
        P("tok", "exp", None),
    )
    out_specs = P(("tok", "exp"), None)
    return jax.shard_map(shards, mesh=mesh, in_specs=in_specs, out_specs=out_specs, check_vma=False)
```
